256 devices in a mesh: seq: 16 (over y, z_hi, core), dp: 16 (over x, z_lo).
Axes of the slice: x: 4, y: 4, z: 8 (z_hi: 2, z_lo: 4; z = z_hi * 4 + z_lo), core: 2. Of those that a mesh axis runs over, the one named last changes fastest.
Arguments:
- inputs: bfloat16 [32768, 1536], P(('dp', 'seq')), parts along dimension 0, may hold values from -6 to 6
- lengths: int32 [16], P('dp'), parts along dimension 0, may hold values from 1024 to 2048
- kernel: float32 [31, 1536], replicated, may hold values from -1 to 1
- gain: float32 [1536], replicated, may hold values from 0.5 to 1.5
- q_weight: bfloat16 [1536, 1024], replicated
- k_weight: bfloat16 [1536, 1024], replicated, may hold values from -0.15625 to 0.15625
- v_weight: bfloat16 [1536, 1024], replicated, may hold values from -0.15625 to 0.15625
- grad_attn: bfloat16 [32768, 1024], P(('dp', 'seq')), parts along dimension 0, may hold values from -6 to 6
Outputs:
- attn: bfloat16 [32768, 1024], P(('dp', 'seq')), parts along dimension 0
- grad_input: bfloat16 [32768, 1536], P(('dp', 'seq')), parts along dimension 0
- grad_kernel: float32 [496, 1536], P('dp'), parts along dimension 0
The draws below stay inside these ranges and needn't reach their ends.
There are 16 independent parts, one for each index of `dp`. The reference program is written for one: setup_inputs(seed, part) draws one part's arguments, and reference() takes and returns one part's arrays. A program takes and returns all parts, laid end to end along the dimension named above; an argument that names none is the same for every part. Nothing has to cross between parts.
All inputs are finite; a program needn't handle non-finite values.
Results may differ from the reference program's by a relative error of at most 0.04.
The reference program's roundings to bfloat16 on the way (of `masked`, `normed`, `weights`, `dout` and `dscores`) count: a program that leaves them out, or rounds other values in their place, can miss the bound.
Values may be sent and summed in bfloat16 or wider, within the bound.
No kernel may reach another device: no remote copies, remote signals or barrier semaphores. Data moves between devices by JAX's collectives and lax.ppermute only.
A program may use at most 128 MiB of HBM per device.

```python
import math
import jax
import jax.numpy as jnp
from jax import lax

D = 1536
HEADS = 16
HDIM = 64
KSIZE = 31
FRAMES = 2048
HD = 1024


def draw_q_weight(key, part):
    key = jax.random.fold_in(key, 7)
    base_key, scale_key = jax.random.split(key)
    base = jax.random.normal(base_key, (D, HEADS * HDIM), jnp.float32) * D ** (-0.5)
    factor = jnp.exp(jax.random.uniform(scale_key, (HEADS,), jnp.float32, math.log(0.5), math.log(2.0)))
    return (base * jnp.repeat(factor, HDIM)[None, :]).astype(jnp.bfloat16)


def shard_levels(own_key, dims, cuts, least, high):
    level, own = 1.0, jax.random.fold_in(own_key, 6)
    for axis_at, shards_of in cuts:
        steps = jnp.exp(jax.random.uniform(jax.random.fold_in(own, axis_at), (shards_of,), jnp.float32, least / len(cuts), high / len(cuts)))
        level = level * jnp.repeat(steps, dims[axis_at] // shards_of).reshape([-1 if axis == axis_at else 1 for axis in range(len(dims))])
    return level


def noise(own_key, shape, scale, reach, shards=(), kind=jnp.bfloat16):
    entries = scale * jax.random.normal(own_key, shape, jnp.float32)
    if shards:
        entries = entries * shard_levels(own_key, shape, shards, -0.22, 0.18)
    return jnp.clip(entries, -reach, reach).astype(kind)


def setup_inputs(seed: int = 0, part: int = 0) -> dict:
    splits = jax.random.split(jax.random.key(seed), 9)
    own_keys = jax.random.split(jax.random.fold_in(splits[8], part), 9)
    inputs = noise(own_keys[0], (FRAMES, D), 1.0, 6.0, ((0, 16),))
    lengths = jax.random.randint(own_keys[1], (1,), FRAMES // 2, FRAMES + 1).astype(jnp.int32)
    kernel = noise(splits[2], (KSIZE, D), KSIZE ** -0.5, 1.0, (), jnp.float32)
    gain = jnp.clip(1.0 + 0.1 * jax.random.normal(splits[3], (D,), jnp.float32), 0.5, 1.5)
    q_weight = draw_q_weight(jax.random.fold_in(splits[8], 71), part)
    k_weight = noise(splits[5], (D, HD), D ** -0.5, 0.15625)
    v_weight = noise(splits[6], (D, HD), D ** -0.5, 0.15625)
    grad_attn = noise(own_keys[7], (FRAMES, HD), 1.0, 6.0, ((0, 16),))
    return {"inputs": inputs, "lengths": lengths, "kernel": kernel, "gain": gain, "q_weight": q_weight, "k_weight": k_weight, "v_weight": v_weight, "grad_attn": grad_attn}


def head_forward(query, key, value, valid):
    frames = query.shape[0]
    groups = query.shape[1] // HDIM
    block = min(512, frames)
    qblocks = query.reshape(frames // block, block, groups, HDIM).astype(jnp.float32)
    keys = key.reshape(frames, groups, HDIM).astype(jnp.float32)
    values = value.reshape(frames, groups, HDIM).astype(jnp.float32)

    def one_block(qblock):
        scores = jnp.einsum('bgd,lgd->gbl', qblock, keys) * HDIM ** (-0.5)
        scores = jnp.where(valid[None, None, :], scores, -1e+30)
        top = lax.optimization_barrier(jnp.max(scores, axis=-1, keepdims=True))
        expo = jnp.exp(scores - top)
        probs = expo / lax.optimization_barrier(jnp.sum(expo, axis=-1, keepdims=True))
        weights = probs.astype(jnp.bfloat16).astype(jnp.float32)
        return jnp.einsum('gbl,lgd->bgd', weights, values).astype(jnp.bfloat16)
    result = lax.map(one_block, qblocks)
    return result.reshape(frames, groups * HDIM)

def head_backward(query, key, value, dout, valid):
    frames = query.shape[0]
    groups = query.shape[1] // HDIM
    block = min(512, frames)
    qblocks = query.reshape(frames // block, block, groups, HDIM).astype(jnp.float32)
    dblocks = dout.reshape(frames // block, block, groups, HDIM).astype(jnp.float32)
    keys = key.reshape(frames, groups, HDIM).astype(jnp.float32)
    values = value.reshape(frames, groups, HDIM).astype(jnp.float32)

    def one_block(carry, pair):
        qblock, dblock = pair
        scores = jnp.einsum('bgd,lgd->gbl', qblock, keys) * HDIM ** (-0.5)
        scores = jnp.where(valid[None, None, :], scores, -1e+30)
        top = lax.optimization_barrier(jnp.max(scores, axis=-1, keepdims=True))
        expo = jnp.exp(scores - top)
        probs = expo / lax.optimization_barrier(jnp.sum(expo, axis=-1, keepdims=True))
        weights = probs.astype(jnp.bfloat16).astype(jnp.float32)
        grad_val = jnp.einsum('gbl,bgd->lgd', weights, dblock)
        dprobs = jnp.einsum('bgd,lgd->gbl', dblock, values)
        delta = lax.optimization_barrier(jnp.sum(probs * dprobs, axis=-1, keepdims=True))
        dscores = (probs * (dprobs - delta) * HDIM ** (-0.5)).astype(jnp.bfloat16).astype(jnp.float32)
        grad_q = jnp.einsum('gbl,lgd->bgd', dscores, keys).astype(jnp.bfloat16)
        grad_k = jnp.einsum('gbl,bgd->lgd', dscores, qblock)
        return ((carry[0] + grad_k, carry[1] + grad_val), grad_q)
    start = (jnp.zeros((frames, groups, HDIM), jnp.float32), jnp.zeros((frames, groups, HDIM), jnp.float32))
    (grad_k, grad_val), grad_q = lax.scan(one_block, start, (qblocks, dblocks))
    width = groups * HDIM
    return (grad_q.reshape(frames, width), grad_k.astype(jnp.bfloat16).reshape(frames, width), grad_val.astype(jnp.bfloat16).reshape(frames, width))

def reference(inputs, lengths, kernel, gain, q_weight, k_weight, v_weight, grad_attn):
    frames = inputs.shape[0]
    half = KSIZE // 2
    positions = jnp.arange(frames, dtype=jnp.int32)
    valid = positions < lengths[0]
    live = valid.astype(jnp.bfloat16)[:, None]
    masked = inputs * live
    padded = jnp.pad(masked.astype(jnp.float32), ((half, half), (0, 0)))
    conv = jnp.zeros((frames, inputs.shape[1]), jnp.float32)
    for tap in range(KSIZE):
        conv = conv + kernel[tap] * padded[tap:tap + frames]
    mixed = inputs.astype(jnp.float32) + conv
    rstd = lax.rsqrt(lax.optimization_barrier(jnp.mean(mixed * mixed, axis=-1, keepdims=True)) + 1e-05)
    normed = (mixed * rstd * gain).astype(jnp.bfloat16)
    query = jnp.dot(normed, q_weight, preferred_element_type=jnp.float32).astype(jnp.bfloat16)
    key = jnp.dot(normed, k_weight, preferred_element_type=jnp.float32).astype(jnp.bfloat16)
    value = jnp.dot(normed, v_weight, preferred_element_type=jnp.float32).astype(jnp.bfloat16)
    heads_out = head_forward(query, key, value, valid)
    attn = heads_out * live
    dout = grad_attn * live
    grad_q, grad_k, grad_val = head_backward(query, key, value, dout, valid)
    contract = (((1,), (1,)), ((), ()))
    grad_normed = lax.dot_general(grad_q, q_weight, contract, preferred_element_type=jnp.float32)
    grad_normed = grad_normed + lax.dot_general(grad_k, k_weight, contract, preferred_element_type=jnp.float32)
    grad_normed = grad_normed + lax.dot_general(grad_val, v_weight, contract, preferred_element_type=jnp.float32)
    scaled = grad_normed * gain
    grad_mixed = rstd * scaled - mixed * rstd ** 3 * lax.optimization_barrier(jnp.mean(scaled * mixed, axis=-1, keepdims=True))
    grad_pad = jnp.pad(grad_mixed, ((half, half), (0, 0)))
    back = jnp.zeros_like(grad_mixed)
    taps = []
    for tap in range(KSIZE):
        back = back + kernel[tap] * grad_pad[2 * half - tap:2 * half - tap + frames]
        taps.append(lax.optimization_barrier(jnp.sum(grad_mixed * padded[tap:tap + frames], axis=0)))
    grad_kernel = jnp.stack(taps, axis=0)
    grad_input = (grad_mixed + live.astype(jnp.float32) * back).astype(jnp.bfloat16)
    return (attn, grad_input, grad_kernel)
```

```python
import functools
import math

import jax
import jax.numpy as jnp
from jax import lax
from jax.experimental import pallas as pl
from jax.experimental.pallas import tpu as pltpu
from jax.sharding import PartitionSpec as P

HEADS = 16
HDIM = 64
KSIZE = 31
PAD = 16
LANES = 128
BF = jnp.bfloat16
F32 = jnp.float32
VMEM = pl.BlockSpec(memory_space=pltpu.VMEM)
SMEM = pl.BlockSpec(memory_space=pltpu.SMEM)
ANY = pl.BlockSpec(memory_space=pl.ANY)


def live_rows(first, rows, length):
    pos = first + lax.broadcasted_iota(jnp.int32, (rows, LANES), 0)
    return (pos < length).astype(F32)


def padded_chunk(lo_ref, x_ref, hi_ref, lanes, mask):
    whole = jnp.concatenate(
        [lo_ref[:, lanes], x_ref[:, lanes], hi_ref[:, lanes]], axis=0
    ).astype(F32)
    return whole * mask if mask is not None else whole


def conv_chunk(padded, taps_ref, lanes, rows, reverse):
    total = None
    for r in range(8):
        acc = None
        for a in range(4):
            o = 8 * a + r
            if o == 0:
                continue
            j = KSIZE - o if reverse else o - 1
            term = taps_ref[j : j + 1, lanes] * padded[8 * a : 8 * a + rows + 8]
            acc = term if acc is None else acc + term
        part = acc[r : r + rows]
        total = part if total is None else total + part
    return total


def chunk(c):
    return pl.ds(pl.multiple_of(c * LANES, LANES), LANES)


def pre_kernel(
    len_ref, first_ref, x_ref, lo_ref, hi_ref, taps_ref, gain_ref, g_ref, wq_ref, wk_ref, wv_ref,
    send_ref, mixed_ref, rstd_ref, w_scr, n_scr, sems,
):
    rows, width = x_ref.shape
    copies = [
        pltpu.make_async_copy(w, w_scr.at[i], sems.at[i])
        for i, w in enumerate((wq_ref, wk_ref, wv_ref))
    ]
    for cp in copies:
        cp.start()
    length = len_ref[0]
    first = first_ref[0]
    mask = live_rows(first - PAD, rows + 2 * PAD, length)

    def conv_step(c, sq):
        lanes = chunk(c)
        padded = padded_chunk(lo_ref, x_ref, hi_ref, lanes, mask)
        conv = conv_chunk(padded, taps_ref, lanes, rows, False)
        mixed = x_ref[:, lanes].astype(F32) + conv
        mixed_ref[:, lanes] = mixed
        return sq + mixed * mixed

    sq = lax.fori_loop(0, width // LANES, conv_step, jnp.zeros((rows, LANES), F32))
    rstd = lax.rsqrt(jnp.sum(sq, axis=-1, keepdims=True) / width + 1e-05)
    rstd_ref[...] = jnp.broadcast_to(rstd, (rows, LANES))
    n_scr[...] = (mixed_ref[...] * rstd * gain_ref[...]).astype(BF)
    live = live_rows(first, rows, length)[:, :HDIM]
    for h in range(HEADS):
        dout = g_ref[:, h * HDIM : (h + 1) * HDIM].astype(F32) * live
        send_ref[h, :, HDIM : 2 * HDIM] = dout.astype(BF)
    for i, at in enumerate((0, 2 * HDIM, 3 * HDIM)):
        copies[i].wait()
        heads = jnp.dot(n_scr[...], w_scr[i], preferred_element_type=F32).astype(BF)
        for h in range(HEADS):
            send_ref[h, :, at : at + HDIM] = heads[:, h * HDIM : (h + 1) * HDIM]


def attn_kernel(len_ref, in_ref, out_ref, kvt_scr, s_scr, e_scr, d_scr, acc_scr, *, block, step):
    frames = in_ref.shape[0]
    length = len_ref[0]
    scale = HDIM ** (-0.5)
    factor = scale * math.log2(math.e)
    half = frames // 2
    kv = in_ref.at[:, 2 * HDIM : 4 * HDIM]
    kvt_scr[...] = kv[...].T
    acc_scr[...] = jnp.zeros_like(acc_scr)
    lane = lax.broadcasted_iota(jnp.int32, (block, LANES), 1)
    nt = (((1,), (1,)), ((), ()))
    steps = frames // step

    def one_block(b, _):
        rows = pl.ds(pl.multiple_of(b * block, block), block)
        qd = in_ref[rows, 0 : 2 * HDIM]
        zero = jnp.zeros_like(qd)
        q0 = jnp.where(lane < HDIM, qd, zero)
        d0 = jnp.where(lane < HDIM, zero, qd)
        top = None
        for i in range(steps):
            keys = slice(i * step, (i + 1) * step)
            s = lax.dot_general(kv[keys, :], q0, nt, preferred_element_type=F32)
            if (i + 1) * step > half:
                pos = i * step + lax.broadcasted_iota(jnp.int32, (step, block), 0)
                s = jnp.where(pos < length, s, -1e30)
            s_scr[keys, :] = s
            part = jnp.max(s.reshape(step // 8, 8, block), axis=0)
            top = part if top is None else jnp.maximum(top, part)
        top = jnp.max(top, axis=0, keepdims=True)
        total = jnp.zeros((8, block), F32)
        out = jnp.zeros((HDIM, block), F32)
        for i in range(steps):
            keys = slice(i * step, (i + 1) * step)
            e = jnp.exp2((s_scr[keys, :] - top) * factor)
            s_scr[keys, :] = e
            eb = e.astype(BF)
            e_scr[keys, :] = eb
            total = total + jnp.sum(e.reshape(step // 8, 8, block), axis=0)
            out = out + jnp.dot(kvt_scr[HDIM:, keys], eb, preferred_element_type=F32)
        inv = 1.0 / jnp.sum(total, axis=0, keepdims=True)
        out = out * inv
        dt = d0.astype(F32).T[HDIM:, :] * inv
        delta = jnp.sum(dt * out, axis=0, keepdims=True)
        dsc = jnp.concatenate([jnp.zeros((HDIM, block), F32), dt], axis=0)
        d0s = dsc.T.astype(BF)
        gq = jnp.zeros((HDIM, block), F32)
        for i in range(steps):
            keys = slice(i * step, (i + 1) * step)
            dp = lax.dot_general(kv[keys, :], d0s, nt, preferred_element_type=F32)
            ds = (s_scr[keys, :] * (dp - delta)).astype(BF)
            gq = gq + jnp.dot(kvt_scr[:HDIM, keys], ds, preferred_element_type=F32)
            acc_scr[keys, :] += jnp.dot(ds, q0, preferred_element_type=F32) + jnp.dot(
                e_scr[keys, :], d0s, preferred_element_type=F32
            )
        both = jnp.concatenate([out, gq * scale], axis=0)
        out_ref[rows, 2 * HDIM : 4 * HDIM] = both.T.astype(BF)
        return 0

    lax.fori_loop(0, frames // block, one_block, 0)
    lane = lax.broadcasted_iota(jnp.int32, (1, LANES), 1)
    fix = jnp.where(lane < HDIM, scale, 1.0)
    out_ref[:, 0 : 2 * HDIM] = (acc_scr[...] * fix).astype(BF)


def back_kernel(
    in_ref, wq_ref, wk_ref, wv_ref, mixed_ref, rstd_ref, gain_ref, gm_ref, first_ref, last_ref
):
    rows, width = mixed_ref.shape
    nt = (((1,), (1,)), ((), ()))
    grad = None
    for w_ref, at in ((wq_ref, 3 * HDIM), (wk_ref, 0), (wv_ref, HDIM)):
        feats = jnp.concatenate([in_ref[h, :, at : at + HDIM] for h in range(HEADS)], axis=1)
        part = lax.dot_general(feats, w_ref[...], nt, preferred_element_type=F32)
        grad = part if grad is None else grad + part
    scaled = grad * gain_ref[...]
    mixed = mixed_ref[...]
    rstd = rstd_ref[:, 0:1]
    mean = jnp.sum(scaled * mixed, axis=-1, keepdims=True) / width
    gm = rstd * scaled - mixed * (rstd * rstd * rstd * mean)
    gm_ref[...] = gm
    first_ref[...] = gm[:PAD].astype(BF)
    last_ref[...] = gm[rows - PAD :].astype(BF)


def taps_kernel(len_ref, first_ref, x_ref, lo_ref, hi_ref, gm_ref, out_ref):
    rows, width = x_ref.shape
    mask = live_rows(first_ref[0] - PAD, rows + 2 * PAD, len_ref[0])

    def step(c, _):
        lanes = chunk(c)
        padded = padded_chunk(lo_ref, x_ref, hi_ref, lanes, mask)
        gm = gm_ref[:, lanes]
        result = [None] * (KSIZE + 1)
        for r in range(8):
            fill = [jnp.zeros((r, LANES), F32)] if r else []
            ext = jnp.concatenate(fill + [gm, jnp.zeros((8 - r, LANES), F32)], axis=0)
            for a in range(4):
                o = 8 * a + r
                if o == 0:
                    continue
                prod = ext * padded[8 * a : 8 * a + rows + 8]
                result[o - 1] = jnp.sum(prod, axis=0, keepdims=True)
        result[KSIZE] = jnp.zeros((1, LANES), F32)
        out_ref[:, lanes] = jnp.concatenate(result, axis=0).astype(BF)
        return 0

    lax.fori_loop(0, width // LANES, step, 0)


def final_kernel(len_ref, first_ref, in_ref, gm_ref, lo_ref, hi_ref, taps_ref, attn_ref, gi_ref):
    rows, width = gm_ref.shape
    live = live_rows(first_ref[0], rows, len_ref[0])

    def step(c, _):
        lanes = chunk(c)
        gm = gm_ref[:, lanes]
        padded = jnp.concatenate(
            [lo_ref[:, lanes].astype(F32), gm, hi_ref[:, lanes].astype(F32)], axis=0
        )
        back = conv_chunk(padded, taps_ref, lanes, rows, True)
        gi_ref[:, lanes] = (gm + live * back).astype(BF)
        return 0

    lax.fori_loop(0, width // LANES, step, 0)
    for h in range(HEADS):
        out = in_ref[h, :, 2 * HDIM : 3 * HDIM].astype(F32) * live[:, :HDIM]
        attn_ref[:, h * HDIM : (h + 1) * HDIM] = out.astype(BF)


def params(mib):
    return pltpu.CompilerParams(vmem_limit_bytes=mib << 20)


def halo(low, high):
    count = lax.axis_size("seq")
    forward = [(i, i + 1) for i in range(count - 1)]
    backward = [(i + 1, i) for i in range(count - 1)]
    return lax.ppermute(low, "seq", forward), lax.ppermute(high, "seq", backward)


def local(inputs, lengths, kernel, gain, q_weight, k_weight, v_weight, grad_attn):
    rows, width = inputs.shape
    count = lax.axis_size("seq")
    frames = rows * count
    feats = HEADS * HDIM
    sds = jax.ShapeDtypeStruct
    first = (lax.axis_index("seq") * rows).astype(jnp.int32).reshape(1)
    gain = gain.reshape(1, width)
    lo, hi = halo(inputs[rows - PAD :], inputs[:PAD])

    send, mixed, rstd = pl.pallas_call(
        pre_kernel,
        name="pre",
        out_shape=(
            sds((HEADS, rows, 4 * HDIM), BF),
            sds((rows, width), F32),
            sds((rows, LANES), F32),
        ),
        in_specs=[SMEM, SMEM] + [VMEM] * 6 + [ANY] * 3,
        out_specs=(VMEM,) * 3,
        scratch_shapes=[
            pltpu.VMEM((3, width, feats), BF),
            pltpu.VMEM((rows, width), BF),
            pltpu.SemaphoreType.DMA((3,)),
        ],
        compiler_params=params(24),
    )(lengths, first, inputs, lo, hi, kernel, gain, grad_attn, q_weight, k_weight, v_weight)

    heads_in = lax.all_to_all(send, "seq", split_axis=0, concat_axis=0, tiled=True)
    block, step = 256, 256
    heads_out = pl.pallas_call(
        functools.partial(attn_kernel, block=block, step=step),
        name="attn",
        out_shape=sds((frames, 4 * HDIM), BF),
        in_specs=[SMEM, VMEM],
        out_specs=VMEM,
        scratch_shapes=[
            pltpu.VMEM((2 * HDIM, frames), BF),
            pltpu.VMEM((frames, block), F32),
            pltpu.VMEM((frames, block), BF),
            pltpu.VMEM((frames, block), BF),
            pltpu.VMEM((frames, LANES), F32),
        ],
        compiler_params=params(24),
    )(lengths, heads_in.reshape(frames, 4 * HDIM))
    grads = lax.all_to_all(
        heads_out.reshape(HEADS, rows, 4 * HDIM), "seq", split_axis=0, concat_axis=0, tiled=True
    )

    gm, gm_first, gm_last = pl.pallas_call(
        back_kernel,
        name="back",
        out_shape=(sds((rows, width), F32), sds((PAD, width), BF), sds((PAD, width), BF)),
        in_specs=[VMEM] * 7,
        out_specs=(VMEM,) * 3,
        compiler_params=params(24),
    )(grads, q_weight, k_weight, v_weight, mixed, rstd, gain)
    gm_lo, gm_hi = halo(gm_last, gm_first)
    taps = pl.pallas_call(
        taps_kernel,
        name="taps",
        out_shape=sds((KSIZE + 1, width), BF),
        in_specs=[SMEM, SMEM] + [VMEM] * 4,
        out_specs=VMEM,
        compiler_params=params(24),
    )(lengths, first, inputs, lo, hi, gm)
    total = taps.astype(F32)
    for bit in (1, 4, 8, 2):
        pairs = [(i, i ^ bit) for i in range(count)]
        mine = total.astype(BF)
        total = mine.astype(F32) + lax.ppermute(mine, "seq", pairs).astype(F32)
    attn, grad_input = pl.pallas_call(
        final_kernel,
        name="final",
        out_shape=(sds((rows, feats), BF), sds((rows, width), BF)),
        in_specs=[SMEM, SMEM] + [VMEM] * 5,
        out_specs=(VMEM,) * 2,
        compiler_params=params(24),
    )(lengths, first, grads, gm, gm_lo, gm_hi, kernel)
    return (attn, grad_input, total[:KSIZE])


def solution(mesh):
    placed = (P(("dp", "seq"), None), P("dp"), P(), P(), P(), P(), P(), P(("dp", "seq"), None))
    return jax.shard_map(
        local,
        mesh=mesh,
        in_specs=placed,
        out_specs=(P(("dp", "seq"), None), P(("dp", "seq"), None), P("dp", None)),
        check_vma=False,
    )
```

```python
import functools
import math

import jax
import jax.numpy as jnp
from jax import lax
from jax.experimental import pallas as pl
from jax.experimental.pallas import tpu as pltpu
from jax.sharding import PartitionSpec as P

HEADS = 16
HDIM = 64
KSIZE = 31
PAD = 16
LANES = 128
BF = jnp.bfloat16
F32 = jnp.float32
VMEM = pl.BlockSpec(memory_space=pltpu.VMEM)
SMEM = pl.BlockSpec(memory_space=pltpu.SMEM)
HBM = pl.BlockSpec(memory_space=pltpu.HBM)


def live_rows(first, rows, length):
    pos = first + lax.broadcasted_iota(jnp.int32, (rows, LANES), 0)
    return ((pos >= 0) & (pos < length)).astype(F32)


def ends(first, near_ref, far_ref, lanes, rows, length):
    odd = lax.rem(first // rows, 2) == 1
    near = near_ref[:, lanes].astype(F32)
    far = far_ref[:, lanes].astype(F32)
    low = jnp.where(odd, near, far) * live_rows(first - PAD, PAD, length)
    high = jnp.where(odd, far, near) * live_rows(first + rows, PAD, length)
    return low, high


def conv_chunk(padded, taps_ref, lanes, rows, reverse):
    total = None
    for r in range(8):
        acc = None
        for a in range(4):
            o = 8 * a + r
            if o == 0:
                continue
            j = KSIZE - o if reverse else o - 1
            term = taps_ref[j : j + 1, lanes] * padded[8 * a : 8 * a + rows + 8]
            acc = term if acc is None else acc + term
        part = acc[r : r + rows]
        total = part if total is None else total + part
    return total


def chunk(c):
    return pl.ds(pl.multiple_of(c * LANES, LANES), LANES)


def early_kernel(
    len_ref, first_ref, x_hbm, taps_hbm, g_hbm, wq_ref, wk_ref, wv_ref,
    conv_ref, w_ref, d_ref, x_ref, taps_ref, g_ref, sems,
):
    rows, width = x_ref.shape
    moves = ((x_hbm, x_ref), (taps_hbm, taps_ref), (g_hbm, g_ref))
    moves += tuple((w, w_ref.at[i]) for i, w in enumerate((wq_ref, wk_ref, wv_ref)))
    copies = [pltpu.make_async_copy(*m, sems.at[i]) for i, m in enumerate(moves)]
    for cp in copies:
        cp.start()
    live = live_rows(first_ref[0], rows, len_ref[0])
    zero = jnp.zeros((PAD, LANES), F32)
    for cp in copies[:3]:
        cp.wait()

    def conv_step(c, _):
        lanes = chunk(c)
        x = x_ref[:, lanes].astype(F32)
        padded = jnp.concatenate([zero, x * live, zero], axis=0)
        conv_ref[:, lanes] = x + conv_chunk(padded, taps_ref, lanes, rows, False)
        return 0

    lax.fori_loop(0, width // LANES, conv_step, 0)
    d_ref[...] = (g_ref[...].astype(F32) * live[:, 0:1]).T.astype(BF).reshape(d_ref.shape)
    for cp in copies[3:]:
        cp.wait()


def edge_convs(low, high, taps_ref, lanes, reverse):
    zero = jnp.zeros((2 * PAD, LANES), F32)
    top = conv_chunk(jnp.concatenate([low, zero], axis=0), taps_ref, lanes, PAD, reverse)
    end = conv_chunk(jnp.concatenate([zero, high], axis=0), taps_ref, lanes, PAD, reverse)
    return top, end


def pre_kernel(
    len_ref, first_ref, conv_ref, near_ref, far_ref, taps_ref, gain_ref, w_ref, d_ref,
    send_ref, mixed_ref, rstd_ref,
):
    rows, width = conv_ref.shape

    def conv_step(c, sq):
        lanes = chunk(c)
        low, high = ends(first_ref[0], near_ref, far_ref, lanes, rows, len_ref[0])
        top, end = edge_convs(low, high, taps_ref, lanes, False)
        mixed = jnp.concatenate(
            [
                conv_ref[:PAD, lanes] + top,
                conv_ref[PAD : rows - PAD, lanes],
                conv_ref[rows - PAD :, lanes] + end,
            ],
            axis=0,
        )
        mixed_ref[:, lanes] = mixed
        return sq + mixed * mixed

    sq = lax.fori_loop(0, width // LANES, conv_step, jnp.zeros((rows, LANES), F32))
    rstd = lax.rsqrt(jnp.sum(sq, axis=-1, keepdims=True) / width + 1e-05)
    rstd_ref[...] = jnp.broadcast_to(rstd, (rows, LANES))
    normed = (mixed_ref[...] * rstd * gain_ref[...]).astype(BF)
    for i in range(3):
        heads = jnp.dot(normed, w_ref[i], preferred_element_type=F32)
        send_ref[:, i * HDIM : (i + 1) * HDIM, :] = heads.T.astype(BF).reshape(HEADS, HDIM, rows)
    send_ref[:, 3 * HDIM :, :] = d_ref[...]


def attn_kernel(
    len_ref, in_ref, out_ref, qt_scr, dt_scr, kvt_scr, kv_scr, s_scr, e_scr, acc_scr,
    *, block, step,
):
    count, _, rows = in_ref.shape
    frames = count * rows
    length = len_ref[0]
    scale = HDIM ** (-0.5)
    factor = scale * math.log2(math.e)
    half = frames // 2
    for s in range(count):
        at = slice(s * rows, (s + 1) * rows)
        qt_scr[:, at] = in_ref[s, 0:HDIM, :]
        kvt = in_ref[s, HDIM : 3 * HDIM, :]
        kvt_scr[:, at] = kvt
        kv_scr[at, :] = kvt.T
        dt_scr[:, at] = in_ref[s, 3 * HDIM :, :]
    acc_scr[...] = jnp.zeros_like(acc_scr)
    steps = frames // step
    zero = jnp.zeros((HDIM, block), BF)

    def one_block(b, _):
        cols = pl.ds(pl.multiple_of(b * block, block), block)
        qt = jnp.concatenate([qt_scr[:, cols], zero], axis=0)
        q0 = qt.T
        top = None
        for i in range(steps):
            keys = slice(i * step, (i + 1) * step)
            s = jnp.dot(kv_scr[keys, :], qt, preferred_element_type=F32)
            if (i + 1) * step > half:
                pos = i * step + lax.broadcasted_iota(jnp.int32, (step, block), 0)
                s = jnp.where(pos < length, s, -1e30)
            s_scr[keys, :] = s
            part = jnp.max(s.reshape(step // 8, 8, block), axis=0)
            top = part if top is None else jnp.maximum(top, part)
        top = jnp.max(top, axis=0, keepdims=True)
        total = jnp.zeros((8, block), F32)
        out = jnp.zeros((HDIM, block), F32)
        for i in range(steps):
            keys = slice(i * step, (i + 1) * step)
            e = jnp.exp2((s_scr[keys, :] - top) * factor)
            s_scr[keys, :] = e
            eb = e.astype(BF)
            e_scr[keys, :] = eb
            total = total + jnp.sum(e.reshape(step // 8, 8, block), axis=0)
            out = out + jnp.dot(kvt_scr[HDIM:, keys], eb, preferred_element_type=F32)
        inv = 1.0 / jnp.sum(total, axis=0, keepdims=True)
        out = out * inv
        dt = dt_scr[:, cols].astype(F32) * inv
        delta = jnp.sum(dt * out, axis=0, keepdims=True)
        dt = jnp.concatenate([zero, dt.astype(BF)], axis=0)
        d0 = dt.T
        gq = jnp.zeros((HDIM, block), F32)
        for i in range(steps):
            keys = slice(i * step, (i + 1) * step)
            dp = jnp.dot(kv_scr[keys, :], dt, preferred_element_type=F32)
            ds = (s_scr[keys, :] * (dp - delta)).astype(BF)
            gq = gq + jnp.dot(kvt_scr[:HDIM, keys], ds, preferred_element_type=F32)
            acc_scr[keys, :] += jnp.dot(ds, q0, preferred_element_type=F32) + jnp.dot(
                e_scr[keys, :], d0, preferred_element_type=F32
            )
        gq = (gq * scale).astype(BF)
        out = out.astype(BF)
        for n in range(block // rows):
            at = slice(n * rows, (n + 1) * rows)
            src = b * (block // rows) + n
            out_ref[src, 0:HDIM, :] = gq[:, at]
            out_ref[src, 3 * HDIM : 4 * HDIM, :] = out[:, at]
        return 0

    lax.fori_loop(0, frames // block, one_block, 0)
    row = lax.broadcasted_iota(jnp.int32, (2 * HDIM, rows), 0)
    fix = jnp.where(row < HDIM, scale, 1.0)
    for s in range(count):
        acc = acc_scr[s * rows : (s + 1) * rows, :]
        out_ref[s, HDIM : 3 * HDIM, :] = (acc.T * fix).astype(BF)


def back_kernel(
    in_ref, wq_ref, wk_ref, wv_ref, mixed_ref, rstd_ref, gain_ref, gm_ref
):
    rows, width = mixed_ref.shape
    nt = (((1,), (1,)), ((), ()))
    grad = None
    for i, w_ref in enumerate((wq_ref, wk_ref, wv_ref)):
        feats = in_ref[:, i * HDIM : (i + 1) * HDIM, :].reshape(HEADS * HDIM, rows).T
        part = lax.dot_general(feats, w_ref[...], nt, preferred_element_type=F32)
        grad = part if grad is None else grad + part
    scaled = grad * gain_ref[...]
    mixed = mixed_ref[...]
    rstd = rstd_ref[:, 0:1]
    mean = jnp.sum(scaled * mixed, axis=-1, keepdims=True) / width
    gm = rstd * scaled - mixed * (rstd * rstd * rstd * mean)
    gm_ref[...] = gm


def taps_kernel(len_ref, first_ref, x_ref, near_ref, far_ref, gm_ref, out_ref):
    rows, width = x_ref.shape
    first = first_ref[0]
    odd = lax.rem(first // rows, 2) == 1
    live = live_rows(first, rows, len_ref[0])

    def step(c, _):
        lanes = chunk(c)
        low, high = ends(first, near_ref, far_ref, lanes, rows, len_ref[0])
        padded = jnp.concatenate([low, x_ref[:, lanes].astype(F32) * live, high], axis=0)
        gm = gm_ref[:, lanes]
        result = [None] * (KSIZE + 1)
        for r in range(8):
            fill = [jnp.zeros((r, LANES), F32)] if r else []
            ext = jnp.concatenate(fill + [gm, jnp.zeros((8 - r, LANES), F32)], axis=0)
            for a in range(4):
                o = 8 * a + r
                if o == 0:
                    continue
                prod = ext * padded[8 * a : 8 * a + rows + 8]
                result[o - 1] = jnp.sum(prod, axis=0, keepdims=True)
        result[KSIZE] = jnp.zeros((1, LANES), F32)
        out_ref[: KSIZE + 1, lanes] = jnp.concatenate(result, axis=0).astype(BF)
        head = gm[:PAD]
        tail = gm[rows - PAD :]
        out_ref[KSIZE + 1 : KSIZE + 1 + PAD, lanes] = jnp.where(odd, head, tail).astype(BF)
        out_ref[KSIZE + 1 + PAD :, lanes] = jnp.where(odd, tail, head).astype(BF)
        return 0

    lax.fori_loop(0, width // LANES, step, 0)


def own_kernel(len_ref, first_ref, in_ref, gm_ref, taps_ref, attn_ref, own_ref):
    rows, width = gm_ref.shape
    live = live_rows(first_ref[0], rows, len_ref[0])
    zero = jnp.zeros((PAD, LANES), F32)

    def step(c, _):
        lanes = chunk(c)
        gm = gm_ref[:, lanes]
        padded = jnp.concatenate([zero, gm, zero], axis=0)
        own_ref[:, lanes] = gm + live * conv_chunk(padded, taps_ref, lanes, rows, True)
        return 0

    lax.fori_loop(0, width // LANES, step, 0)
    out = in_ref[:, 3 * HDIM : 4 * HDIM, :].reshape(HEADS * HDIM, rows).T
    attn_ref[...] = (out.astype(F32) * live[:, 0:1]).astype(BF)


def final_kernel(
    len_ref, first_ref, own_ref, near_ref, far_ref, taps_ref, mine_ref, gi_ref, gk_ref,
    *, frames,
):
    rows, width = own_ref.shape
    first = first_ref[0]
    live = live_rows(first, rows, len_ref[0])
    near_edge = near_ref.at[KSIZE + 1 : KSIZE + 1 + PAD]
    far_edge = far_ref.at[KSIZE + 1 :]

    def step(c, _):
        lanes = chunk(c)
        low, high = ends(first, near_edge, far_edge, lanes, rows, frames)
        top, end = edge_convs(low, high, taps_ref, lanes, True)
        gi_ref[:PAD, lanes] = (own_ref[:PAD, lanes] + live[:PAD] * top).astype(BF)
        gi_ref[PAD : rows - PAD, lanes] = own_ref[PAD : rows - PAD, lanes].astype(BF)
        gi_ref[rows - PAD :, lanes] = (
            own_ref[rows - PAD :, lanes] + live[rows - PAD :] * end
        ).astype(BF)
        gk_ref[:, lanes] = mine_ref[:KSIZE, lanes].astype(F32) + far_ref[:KSIZE, lanes].astype(F32)
        return 0

    lax.fori_loop(0, width // LANES, step, 0)


def params(mib):
    return pltpu.CompilerParams(vmem_limit_bytes=mib << 20)


def cost(us):
    return pl.CostEstimate(flops=int(us * 1.1e9), bytes_accessed=1024, transcendentals=0)


def local(inputs, lengths, kernel, gain, q_weight, k_weight, v_weight, grad_attn):
    rows, width = inputs.shape
    count = lax.axis_size("seq")
    frames = rows * count
    feats = HEADS * HDIM
    sds = jax.ShapeDtypeStruct
    here = lax.axis_index("seq")
    odd = lax.rem(here, 2)
    first = (here * rows).astype(jnp.int32).reshape(1)
    gain = gain.reshape(1, width)

    def peer(mine, move):
        return lax.ppermute(mine, "seq", [(i, move(i)) for i in range(count)])

    def near(mine):
        return peer(mine, lambda i: i ^ 1)

    def far(mine):
        return peer(mine, lambda i: (i + 1 if i % 2 else i - 1) % count)

    a2a = functools.partial(
        lax.all_to_all, axis_name="seq", split_axis=0, concat_axis=0, tiled=True
    )
    x_far = far(lax.dynamic_slice_in_dim(inputs, odd * (rows - PAD), PAD))
    x_near = near(lax.dynamic_slice_in_dim(inputs, (1 - odd) * (rows - PAD), PAD))

    def in_hbm(array):
        return pltpu.with_memory_space_constraint(array, pltpu.HBM)

    own, weights, douts = pl.pallas_call(
        early_kernel,
        name="early",
        out_shape=(
            pltpu.VMEM((rows, width), F32),
            pltpu.VMEM((3, width, feats), BF),
            pltpu.VMEM((HEADS, HDIM, rows), BF),
        ),
        in_specs=[SMEM, SMEM] + [HBM] * 6,
        out_specs=(VMEM,) * 3,
        scratch_shapes=[
            pltpu.VMEM((rows, width), BF),
            pltpu.VMEM((KSIZE, width), F32),
            pltpu.VMEM((rows, feats), BF),
            pltpu.SemaphoreType.DMA((6,)),
        ],
        compiler_params=params(16),
        cost_estimate=cost(6),
    )(lengths, first, *(in_hbm(a) for a in (inputs, kernel, grad_attn, q_weight, k_weight, v_weight)))
    send, mixed, rstd = pl.pallas_call(
        pre_kernel,
        name="pre",
        out_shape=(
            sds((HEADS, 4 * HDIM, rows), BF),
            sds((rows, width), F32),
            sds((rows, LANES), F32),
        ),
        in_specs=[SMEM, SMEM] + [VMEM] * 7,
        out_specs=(VMEM,) * 3,
        compiler_params=params(16),
        cost_estimate=cost(3),
    )(lengths, first, own, x_near, x_far, kernel, gain, weights, douts)

    block, step = 512, 1024
    heads_out = pl.pallas_call(
        functools.partial(attn_kernel, block=block, step=step),
        name="attn",
        out_shape=sds((HEADS, 4 * HDIM, rows), BF),
        in_specs=[SMEM, VMEM],
        out_specs=VMEM,
        scratch_shapes=[
            pltpu.VMEM((HDIM, frames), BF),
            pltpu.VMEM((HDIM, frames), BF),
            pltpu.VMEM((2 * HDIM, frames), BF),
            pltpu.VMEM((frames, 2 * HDIM), BF),
            pltpu.VMEM((frames, block), F32),
            pltpu.VMEM((frames, block), BF),
            pltpu.VMEM((frames, 2 * HDIM), F32),
        ],
        compiler_params=params(32),
        cost_estimate=cost(17),
    )(lengths, a2a(send))
    grads = a2a(heads_out)

    gm = pl.pallas_call(
        back_kernel,
        name="back",
        out_shape=sds((rows, width), F32),
        in_specs=[VMEM] * 7,
        out_specs=VMEM,
        compiler_params=params(16),
        cost_estimate=cost(4),
    )(grads, q_weight, k_weight, v_weight, mixed, rstd, gain)
    taps = pl.pallas_call(
        taps_kernel,
        name="taps",
        out_shape=sds((KSIZE + 1 + 2 * PAD, width), BF),
        in_specs=[SMEM, SMEM] + [VMEM] * 4,
        out_specs=VMEM,
        compiler_params=params(16),
        cost_estimate=cost(3),
    )(lengths, first, inputs, x_near, x_far, gm)

    got = near(taps[: KSIZE + 1 + PAD])
    total = taps[: KSIZE + 1].astype(F32) + got[: KSIZE + 1].astype(F32)
    for bit in (4, 8):
        mine = total.astype(BF)
        total = mine.astype(F32) + peer(mine, lambda i: i ^ bit).astype(F32)
    mine = jnp.concatenate([total.astype(BF), taps[KSIZE + 1 + PAD :]], axis=0)
    last = far(mine)
    attn, own_gi = pl.pallas_call(
        own_kernel,
        name="own",
        out_shape=(sds((rows, feats), BF), sds((rows, width), F32)),
        in_specs=[SMEM, SMEM] + [VMEM] * 3,
        out_specs=(VMEM,) * 2,
        compiler_params=params(16),
        cost_estimate=cost(3),
    )(lengths, first, grads, gm, kernel)
    grad_input, grad_kernel = pl.pallas_call(
        functools.partial(final_kernel, frames=frames),
        name="final",
        out_shape=(sds((rows, width), BF), sds((KSIZE, width), F32)),
        in_specs=[SMEM, SMEM] + [VMEM] * 5,
        out_specs=(VMEM,) * 2,
        compiler_params=params(16),
        cost_estimate=cost(1),
    )(lengths, first, own_gi, got, last, kernel, mine)
    return (attn, grad_input, grad_kernel)


def solution(mesh):
    placed = (P(("dp", "seq"), None), P("dp"), P(), P(), P(), P(), P(), P(("dp", "seq"), None))
    return jax.shard_map(
        local,
        mesh=mesh,
        in_specs=placed,
        out_specs=(P(("dp", "seq"), None), P(("dp", "seq"), None), P("dp", None)),
        check_vma=False,
    )
```

```python
import functools
import math

import jax
import jax.numpy as jnp
from jax import lax
from jax.experimental import pallas as pl
from jax.experimental.pallas import tpu as pltpu
from jax.sharding import PartitionSpec as P

HEADS = 16
HDIM = 64
KSIZE = 31
PAD = 16
LANES = 128
BF = jnp.bfloat16
F32 = jnp.float32
VMEM = pl.BlockSpec(memory_space=pltpu.VMEM)
SMEM = pl.BlockSpec(memory_space=pltpu.SMEM)
HBM = pl.BlockSpec(memory_space=pltpu.HBM)


def live_rows(first, rows, length):
    pos = first + lax.broadcasted_iota(jnp.int32, (rows, LANES), 0)
    return ((pos >= 0) & (pos < length)).astype(F32)


def ends(first, near_ref, far_ref, lanes, rows, length):
    odd = lax.rem(first // rows, 2) == 1
    near = near_ref[:, lanes].astype(F32)
    far = far_ref[:, lanes].astype(F32)
    low = jnp.where(odd, near, far) * live_rows(first - PAD, PAD, length)
    high = jnp.where(odd, far, near) * live_rows(first + rows, PAD, length)
    return low, high


def conv_chunk(padded, taps_ref, lanes, rows, reverse):
    total = None
    for r in range(8):
        acc = None
        for a in range(4):
            o = 8 * a + r
            if o == 0:
                continue
            j = KSIZE - o if reverse else o - 1
            term = taps_ref[j : j + 1, lanes] * padded[8 * a : 8 * a + rows + 8]
            acc = term if acc is None else acc + term
        part = acc[r : r + rows]
        total = part if total is None else total + part
    return total


def chunk(c):
    return pl.ds(pl.multiple_of(c * LANES, LANES), LANES)


def early_kernel(
    len_ref, first_ref, x_hbm, taps_hbm, g_hbm, wq_ref, wk_ref, wv_ref,
    conv_ref, w_ref, d_ref, x_ref, taps_ref, g_ref, sems,
):
    rows, width = x_ref.shape
    moves = ((x_hbm, x_ref), (taps_hbm, taps_ref), (g_hbm, g_ref))
    moves += tuple((w, w_ref.at[i]) for i, w in enumerate((wq_ref, wk_ref, wv_ref)))
    copies = [pltpu.make_async_copy(*m, sems.at[i]) for i, m in enumerate(moves)]
    for cp in copies:
        cp.start()
    live = live_rows(first_ref[0], rows, len_ref[0])
    zero = jnp.zeros((PAD, LANES), F32)
    for cp in copies[:3]:
        cp.wait()

    def conv_step(c, _):
        lanes = chunk(c)
        x = x_ref[:, lanes].astype(F32)
        padded = jnp.concatenate([zero, x * live, zero], axis=0)
        conv_ref[:, lanes] = x + conv_chunk(padded, taps_ref, lanes, rows, False)
        return 0

    lax.fori_loop(0, width // LANES, conv_step, 0)
    d_ref[...] = (g_ref[...].astype(F32) * live[:, 0:1]).T.astype(BF).reshape(d_ref.shape)
    for cp in copies[3:]:
        cp.wait()


def edge_convs(low, high, taps_ref, lanes, reverse):
    zero = jnp.zeros((2 * PAD, LANES), F32)
    top = conv_chunk(jnp.concatenate([low, zero], axis=0), taps_ref, lanes, PAD, reverse)
    end = conv_chunk(jnp.concatenate([zero, high], axis=0), taps_ref, lanes, PAD, reverse)
    return top, end


def pre_kernel(
    len_ref, first_ref, conv_ref, near_ref, far_ref, taps_ref, gain_ref, w_ref, d_ref,
    send_ref, mixed_ref, rstd_ref,
):
    rows, width = conv_ref.shape

    def conv_step(c, sq):
        lanes = chunk(c)
        low, high = ends(first_ref[0], near_ref, far_ref, lanes, rows, len_ref[0])
        top, end = edge_convs(low, high, taps_ref, lanes, False)
        mixed = jnp.concatenate(
            [
                conv_ref[:PAD, lanes] + top,
                conv_ref[PAD : rows - PAD, lanes],
                conv_ref[rows - PAD :, lanes] + end,
            ],
            axis=0,
        )
        mixed_ref[:, lanes] = mixed
        return sq + mixed * mixed

    sq = lax.fori_loop(0, width // LANES, conv_step, jnp.zeros((rows, LANES), F32))
    rstd = lax.rsqrt(jnp.sum(sq, axis=-1, keepdims=True) / width + 1e-05)
    rstd_ref[...] = jnp.broadcast_to(rstd, (rows, LANES))
    normed = (mixed_ref[...] * rstd * gain_ref[...]).astype(BF)
    for i in range(3):
        heads = jnp.dot(normed, w_ref[i], preferred_element_type=F32)
        send_ref[:, i * HDIM : (i + 1) * HDIM, :] = heads.T.astype(BF).reshape(HEADS, HDIM, rows)
    send_ref[:, 3 * HDIM :, :] = d_ref[...]


def attn_kernel(
    len_ref, in_ref, out_ref, qt_scr, dt_scr, kvt_scr, kv_scr, s_scr, e_scr, acc_scr,
    *, block, sstep, step,
):
    count, _, rows = in_ref.shape
    frames = count * rows
    length = len_ref[0]
    scale = HDIM ** (-0.5)
    factor = scale * math.log2(math.e)
    half = frames // 2
    steps = frames // step
    blocks = frames // block
    for s in range(count):
        at = slice(s * rows, (s + 1) * rows)
        qt_scr[:, at] = in_ref[s, 0:HDIM, :]
        kvt = in_ref[s, HDIM : 3 * HDIM, :]
        kvt_scr[:, at] = kvt
        kv_scr[at, :] = kvt.T
        dt_scr[:, at] = in_ref[s, 3 * HDIM :, :]
    acc_scr[...] = jnp.zeros_like(acc_scr)
    zero = jnp.zeros((HDIM, block), BF)
    none = jnp.zeros((HDIM, block), F32)

    def query(b):
        return jnp.concatenate([qt_scr[:, b * block : (b + 1) * block], zero], axis=0)

    def scores(b):
        qt = query(b)
        top = None
        for i in range(frames // sstep):
            keys = slice(i * sstep, (i + 1) * sstep)
            s = jnp.dot(kv_scr[keys, :], qt, preferred_element_type=F32)
            if (i + 1) * sstep > half:
                pos = i * sstep + lax.broadcasted_iota(jnp.int32, (sstep, block), 0)
                s = jnp.where(pos < length, s, -1e30)
            s_scr[b % 2, keys, :] = s
            part = jnp.max(s.reshape(sstep // 8, 8, block), axis=0)
            top = part if top is None else jnp.maximum(top, part)
        return jnp.max(top, axis=0, keepdims=True)

    def forward(b, i, top, total, out):
        keys = slice(i * step, (i + 1) * step)
        e = jnp.exp2((s_scr[b % 2, keys, :] - top) * factor)
        s_scr[b % 2, keys, :] = e
        eb = e.astype(BF)
        e_scr[b % 2, keys, :] = eb
        total = total + jnp.sum(e.reshape(step // 8, 8, block), axis=0)
        return total, out + jnp.dot(kvt_scr[HDIM:, keys], eb, preferred_element_type=F32)

    def between(b, total, out):
        inv = 1.0 / jnp.sum(total, axis=0, keepdims=True)
        out = out * inv
        dt = dt_scr[:, b * block : (b + 1) * block].astype(F32) * inv
        delta = jnp.sum(dt * out, axis=0, keepdims=True)
        return out, delta, jnp.concatenate([zero, dt.astype(BF)], axis=0)

    def backward(b, i, q0, d0, dt, delta, gq):
        keys = slice(i * step, (i + 1) * step)
        dp = jnp.dot(kv_scr[keys, :], dt, preferred_element_type=F32)
        ds = (s_scr[b % 2, keys, :] * (dp - delta)).astype(BF)
        acc_scr[keys, :] += jnp.dot(ds, q0, preferred_element_type=F32) + jnp.dot(
            e_scr[b % 2, keys, :], d0, preferred_element_type=F32
        )
        return gq + jnp.dot(kvt_scr[:HDIM, keys], ds, preferred_element_type=F32)

    state = None
    for b in range(blocks + 1):
        total, ahead, gq = jnp.zeros((8, block), F32), none, none
        if b < blocks:
            top = scores(b)
        if b > 0:
            out, delta, dt = state
            q0, d0 = query(b - 1).T, dt.T
        for i in range(steps):
            if b < blocks:
                total, ahead = forward(b, i, top, total, ahead)
            if b > 0:
                gq = backward(b - 1, i, q0, d0, dt, delta, gq)
        if b < blocks:
            state = between(b, total, ahead)
        if b > 0:
            gq = (gq * scale).astype(BF)
            out = out.astype(BF)
            for n in range(block // rows):
                at = slice(n * rows, (n + 1) * rows)
                dest = (b - 1) * (block // rows) + n
                out_ref[dest, 0:HDIM, :] = gq[:, at]
                out_ref[dest, 3 * HDIM : 4 * HDIM, :] = out[:, at]
    row = lax.broadcasted_iota(jnp.int32, (2 * HDIM, rows), 0)
    fix = jnp.where(row < HDIM, scale, 1.0)
    for s in range(count):
        acc = acc_scr[s * rows : (s + 1) * rows, :]
        out_ref[s, HDIM : 3 * HDIM, :] = (acc.T * fix).astype(BF)


def back_kernel(
    in_ref, wq_ref, wk_ref, wv_ref, mixed_ref, rstd_ref, gain_ref, gm_ref
):
    rows, width = mixed_ref.shape
    nt = (((1,), (1,)), ((), ()))
    grad = None
    for i, w_ref in enumerate((wq_ref, wk_ref, wv_ref)):
        feats = in_ref[:, i * HDIM : (i + 1) * HDIM, :].reshape(HEADS * HDIM, rows).T
        part = lax.dot_general(feats, w_ref[...], nt, preferred_element_type=F32)
        grad = part if grad is None else grad + part
    scaled = grad * gain_ref[...]
    mixed = mixed_ref[...]
    rstd = rstd_ref[:, 0:1]
    mean = jnp.sum(scaled * mixed, axis=-1, keepdims=True) / width
    gm = rstd * scaled - mixed * (rstd * rstd * rstd * mean)
    gm_ref[...] = gm


def taps_kernel(
    len_ref, first_ref, half_ref, x_ref, near_ref, far_ref, gm_ref, keep_ref, give_ref, edge_ref
):
    rows, width = x_ref.shape
    first = first_ref[0]
    odd = lax.rem(first // rows, 2) == 1
    live = live_rows(first, rows, len_ref[0])
    count = width // 2 // LANES

    def terms(lanes):
        low, high = ends(first, near_ref, far_ref, lanes, rows, len_ref[0])
        padded = jnp.concatenate([low, x_ref[:, lanes].astype(F32) * live, high], axis=0)
        gm = gm_ref[:, lanes]
        result = [None] * (KSIZE + 1)
        for r in range(8):
            fill = [jnp.zeros((r, LANES), F32)] if r else []
            ext = jnp.concatenate(fill + [gm, jnp.zeros((8 - r, LANES), F32)], axis=0)
            for a in range(4):
                o = 8 * a + r
                if o == 0:
                    continue
                prod = ext * padded[8 * a : 8 * a + rows + 8]
                result[o - 1] = jnp.sum(prod, axis=0, keepdims=True)
        result[KSIZE] = jnp.zeros((1, LANES), F32)
        return jnp.concatenate(result, axis=0)

    def step(c, _):
        keep_ref[:, chunk(c)] = terms(chunk(c + half_ref[0] * count))
        give_ref[: KSIZE + 1, chunk(c)] = terms(chunk(c + (1 - half_ref[0]) * count)).astype(BF)
        for n in range(2):
            lanes = chunk(c + n * count)
            head = gm_ref[:PAD, lanes]
            tail = gm_ref[rows - PAD :, lanes]
            at = n * PAD
            give_ref[KSIZE + 1 + at : KSIZE + 1 + at + PAD, chunk(c)] = jnp.where(
                odd, head, tail
            ).astype(BF)
            edge_ref[at : at + PAD, chunk(c)] = jnp.where(odd, tail, head).astype(BF)
        return 0

    lax.fori_loop(0, count, step, 0)


def own_kernel(len_ref, first_ref, in_ref, gm_ref, taps_ref, attn_ref, own_ref):
    rows, width = gm_ref.shape
    live = live_rows(first_ref[0], rows, len_ref[0])
    zero = jnp.zeros((PAD, LANES), F32)

    def step(c, _):
        lanes = chunk(c)
        gm = gm_ref[:, lanes]
        padded = jnp.concatenate([zero, gm, zero], axis=0)
        own_ref[:, lanes] = gm + live * conv_chunk(padded, taps_ref, lanes, rows, True)
        return 0

    lax.fori_loop(0, width // LANES, step, 0)
    out = in_ref[:, 3 * HDIM : 4 * HDIM, :].reshape(HEADS * HDIM, rows).T
    attn_ref[...] = (out.astype(F32) * live[:, 0:1]).astype(BF)


def final_kernel(
    len_ref, first_ref, own_ref, near_ref, far_ref, taps_ref, gi_ref, *, frames,
):
    rows, width = own_ref.shape
    first = first_ref[0]
    live = live_rows(first, rows, len_ref[0])
    count = width // 2 // LANES

    def step(c, _):
        for n in range(2):
            lanes = chunk(c + n * count)
            at = KSIZE + 1 + n * PAD
            low, high = ends(
                first, near_ref.at[at : at + PAD], far_ref.at[at : at + PAD], chunk(c), rows, frames
            )
            top, end = edge_convs(low, high, taps_ref, lanes, True)
            gi_ref[:PAD, lanes] = (own_ref[:PAD, lanes] + live[:PAD] * top).astype(BF)
            gi_ref[PAD : rows - PAD, lanes] = own_ref[PAD : rows - PAD, lanes].astype(BF)
            gi_ref[rows - PAD :, lanes] = (
                own_ref[rows - PAD :, lanes] + live[rows - PAD :] * end
            ).astype(BF)
        return 0

    lax.fori_loop(0, count, step, 0)


def params(mib):
    return pltpu.CompilerParams(vmem_limit_bytes=mib << 20)


def cost(us):
    return pl.CostEstimate(flops=int(us * 1.1e9), bytes_accessed=1024, transcendentals=0)


def local(inputs, lengths, kernel, gain, q_weight, k_weight, v_weight, grad_attn):
    rows, width = inputs.shape
    count = lax.axis_size("seq")
    frames = rows * count
    feats = HEADS * HDIM
    sds = jax.ShapeDtypeStruct
    here = lax.axis_index("seq")
    odd = lax.rem(here, 2)
    first = (here * rows).astype(jnp.int32).reshape(1)
    gain = gain.reshape(1, width)

    def peer(mine, move):
        return lax.ppermute(mine, "seq", [(i, move(i)) for i in range(count)])

    def near(mine):
        return peer(mine, lambda i: i ^ 1)

    def far(mine):
        return peer(mine, lambda i: (i + 1 if i % 2 else i - 1) % count)

    a2a = functools.partial(
        lax.all_to_all, axis_name="seq", split_axis=0, concat_axis=0, tiled=True
    )
    x_far = far(lax.dynamic_slice_in_dim(inputs, odd * (rows - PAD), PAD))
    x_near = near(lax.dynamic_slice_in_dim(inputs, (1 - odd) * (rows - PAD), PAD))

    def in_hbm(array):
        return pltpu.with_memory_space_constraint(array, pltpu.HBM)

    own, weights, douts = pl.pallas_call(
        early_kernel,
        name="early",
        out_shape=(
            pltpu.VMEM((rows, width), F32),
            pltpu.VMEM((3, width, feats), BF),
            pltpu.VMEM((HEADS, HDIM, rows), BF),
        ),
        in_specs=[SMEM, SMEM] + [HBM] * 6,
        out_specs=(VMEM,) * 3,
        scratch_shapes=[
            pltpu.VMEM((rows, width), BF),
            pltpu.VMEM((KSIZE, width), F32),
            pltpu.VMEM((rows, feats), BF),
            pltpu.SemaphoreType.DMA((6,)),
        ],
        compiler_params=params(16),
        cost_estimate=cost(6),
    )(lengths, first, *(in_hbm(a) for a in (inputs, kernel, grad_attn, q_weight, k_weight, v_weight)))
    send, mixed, rstd = pl.pallas_call(
        pre_kernel,
        name="pre",
        out_shape=(
            sds((HEADS, 4 * HDIM, rows), BF),
            sds((rows, width), F32),
            sds((rows, LANES), F32),
        ),
        in_specs=[SMEM, SMEM] + [VMEM] * 7,
        out_specs=(VMEM,) * 3,
        compiler_params=params(16),
        cost_estimate=cost(3),
    )(lengths, first, own, x_near, x_far, kernel, gain, weights, douts)

    block, sstep, step = 512, 1024, 512
    heads_out = pl.pallas_call(
        functools.partial(attn_kernel, block=block, sstep=sstep, step=step),
        name="attn",
        out_shape=sds((HEADS, 4 * HDIM, rows), BF),
        in_specs=[SMEM, VMEM],
        out_specs=VMEM,
        scratch_shapes=[
            pltpu.VMEM((HDIM, frames), BF),
            pltpu.VMEM((HDIM, frames), BF),
            pltpu.VMEM((2 * HDIM, frames), BF),
            pltpu.VMEM((frames, 2 * HDIM), BF),
            pltpu.VMEM((2, frames, block), F32),
            pltpu.VMEM((2, frames, block), BF),
            pltpu.VMEM((frames, 2 * HDIM), F32),
        ],
        compiler_params=params(32),
        cost_estimate=cost(17),
    )(lengths, a2a(send))
    grads = a2a(heads_out)

    gm = pl.pallas_call(
        back_kernel,
        name="back",
        out_shape=sds((rows, width), F32),
        in_specs=[VMEM] * 7,
        out_specs=VMEM,
        compiler_params=params(16),
        cost_estimate=cost(4),
    )(grads, q_weight, k_weight, v_weight, mixed, rstd, gain)
    here, gm = lax.optimization_barrier((here, gm))
    half = ((here ^ (here >> 1)) & 1).astype(jnp.int32)
    keep, give, edge = pl.pallas_call(
        taps_kernel,
        name="taps",
        out_shape=(
            sds((KSIZE + 1, width // 2), F32),
            sds((KSIZE + 1 + 2 * PAD, width // 2), BF),
            sds((2 * PAD, width // 2), BF),
        ),
        in_specs=[SMEM] * 3 + [VMEM] * 4,
        out_specs=(VMEM,) * 3,
        compiler_params=params(16),
        cost_estimate=cost(3),
    )(lengths, first, half.reshape(1), inputs, x_near, x_far, gm)

    got = near(give)
    mine = (keep + got[: KSIZE + 1].astype(F32)).astype(BF)
    one, two, three = (peer(mine, lambda i: i ^ bits).astype(F32) for bits in (4, 8, 12))
    mine = ((mine.astype(F32) + one) + (two + three)).astype(BF)
    last = far(jnp.concatenate([mine, edge], axis=0))
    attn, own_gi = pl.pallas_call(
        own_kernel,
        name="own",
        out_shape=(sds((rows, feats), BF), sds((rows, width), F32)),
        in_specs=[SMEM, SMEM] + [VMEM] * 3,
        out_specs=(VMEM,) * 2,
        compiler_params=params(16),
        cost_estimate=cost(3),
    )(lengths, first, grads, gm, kernel)
    mine = (mine.astype(F32) + last[: KSIZE + 1].astype(F32)).astype(BF)
    other = near(mine)
    grad_input = pl.pallas_call(
        functools.partial(final_kernel, frames=frames),
        name="final",
        out_shape=sds((rows, width), BF),
        in_specs=[SMEM, SMEM] + [VMEM] * 4,
        out_specs=VMEM,
        compiler_params=params(16),
        cost_estimate=cost(1),
    )(lengths, first, own_gi, got, last, kernel)
    left = jnp.where(half == 0, mine, other)
    right = jnp.where(half == 0, other, mine)
    grad_kernel = jnp.concatenate([left, right], axis=1)[:KSIZE].astype(F32)
    return (attn, grad_input, grad_kernel)


def solution(mesh):
    placed = (P(("dp", "seq"), None), P("dp"), P(), P(), P(), P(), P(), P(("dp", "seq"), None))
    return jax.shard_map(
        local,
        mesh=mesh,
        in_specs=placed,
        out_specs=(P(("dp", "seq"), None), P(("dp", "seq"), None), P("dp", None)),
        check_vma=False,
    )
```

```python
import functools
import math

import jax
import jax.numpy as jnp
from jax import lax
from jax.experimental import pallas as pl
from jax.experimental.pallas import tpu as pltpu
from jax.sharding import PartitionSpec as P

HEADS = 16
HDIM = 64
KSIZE = 31
PAD = 16
LANES = 128
BF = jnp.bfloat16
F32 = jnp.float32
VMEM = pl.BlockSpec(memory_space=pltpu.VMEM)
SMEM = pl.BlockSpec(memory_space=pltpu.SMEM)
HBM = pl.BlockSpec(memory_space=pltpu.HBM)
ANY = pl.BlockSpec(memory_space=pl.ANY)


def live_rows(first, rows, length):
    pos = first + lax.broadcasted_iota(jnp.int32, (rows, LANES), 0)
    return ((pos >= 0) & (pos < length)).astype(F32)


def ends(first, near_ref, far_ref, lanes, rows, length):
    odd = lax.rem(first // rows, 2) == 1
    near = near_ref[:, lanes].astype(F32)
    far = far_ref[:, lanes].astype(F32)
    low = jnp.where(odd, near, far) * live_rows(first - PAD, PAD, length)
    high = jnp.where(odd, far, near) * live_rows(first + rows, PAD, length)
    return low, high


def conv_chunk(padded, taps_ref, lanes, rows, reverse):
    total = None
    for r in range(8):
        acc = None
        for a in range(4):
            o = 8 * a + r
            if o == 0:
                continue
            j = KSIZE - o if reverse else o - 1
            term = taps_ref[j : j + 1, lanes] * padded[8 * a : 8 * a + rows + 8]
            acc = term if acc is None else acc + term
        part = acc[r : r + rows]
        total = part if total is None else total + part
    return total


def chunk(c):
    return pl.ds(pl.multiple_of(c * LANES, LANES), LANES)


def dout_kernel(len_ref, first_ref, g_ref, out_ref):
    live = live_rows(first_ref[0], g_ref.shape[0], len_ref[0])
    out_ref[...] = (g_ref[...].astype(F32) * live[:, 0:1]).T.astype(BF)


def early_kernel(
    len_ref, first_ref, x_hbm, taps_hbm, wq_ref, wk_ref, wv_ref,
    conv_ref, w_ref, x_ref, taps_ref, sems,
):
    rows, width = x_ref.shape
    moves = ((x_hbm, x_ref), (taps_hbm, taps_ref))
    moves += tuple((w, w_ref.at[i]) for i, w in enumerate((wq_ref, wk_ref, wv_ref)))
    copies = [pltpu.make_async_copy(*m, sems.at[i]) for i, m in enumerate(moves)]
    for cp in copies:
        cp.start()
    live = live_rows(first_ref[0], rows, len_ref[0])
    zero = jnp.zeros((PAD, LANES), F32)
    for cp in copies[:2]:
        cp.wait()

    def conv_step(c, _):
        lanes = chunk(c)
        x = x_ref[:, lanes].astype(F32)
        padded = jnp.concatenate([zero, x * live, zero], axis=0)
        conv_ref[:, lanes] = x + conv_chunk(padded, taps_ref, lanes, rows, False)
        return 0

    lax.fori_loop(0, width // LANES, conv_step, 0)
    for cp in copies[2:]:
        cp.wait()


def edge_convs(low, high, taps_ref, lanes, reverse):
    zero = jnp.zeros((2 * PAD, LANES), F32)
    top = conv_chunk(jnp.concatenate([low, zero], axis=0), taps_ref, lanes, PAD, reverse)
    end = conv_chunk(jnp.concatenate([zero, high], axis=0), taps_ref, lanes, PAD, reverse)
    return top, end


def pre_kernel(
    len_ref, first_ref, conv_ref, near_ref, far_ref, taps_ref, gain_ref, w_ref, d_ref,
    send_ref, all_ref, mixed_ref, rstd_ref,
):
    rows, width = conv_ref.shape

    def conv_step(c, sq):
        lanes = chunk(c)
        low, high = ends(first_ref[0], near_ref, far_ref, lanes, rows, len_ref[0])
        top, end = edge_convs(low, high, taps_ref, lanes, False)
        mixed = jnp.concatenate(
            [
                conv_ref[:PAD, lanes] + top,
                conv_ref[PAD : rows - PAD, lanes],
                conv_ref[rows - PAD :, lanes] + end,
            ],
            axis=0,
        )
        mixed_ref[:, lanes] = mixed
        return sq + mixed * mixed

    sq = lax.fori_loop(0, width // LANES, conv_step, jnp.zeros((rows, LANES), F32))
    rstd = lax.rsqrt(jnp.sum(sq, axis=-1, keepdims=True) / width + 1e-05)
    rstd_ref[...] = jnp.broadcast_to(rstd, (rows, LANES))
    normed = (mixed_ref[...] * rstd * gain_ref[...]).astype(BF)
    for i in range(3):
        heads = jnp.dot(normed, w_ref[i], preferred_element_type=F32)
        heads = heads.T.astype(BF).reshape(HEADS, HDIM, rows)
        send_ref[:, i * HDIM : (i + 1) * HDIM, :] = heads
        all_ref[:, i * HDIM : (i + 1) * HDIM, :] = heads
    all_ref[:, 3 * HDIM :, :] = d_ref[...]


def attn_kernel(
    len_ref, late_ref, part_hbm, whole_hbm, d_hbm, out_ref, in_ref, qt_scr, dt_scr, kvt_scr, kv_scr,
    s_scr, e_scr, acc_scr, sems, *, block, sstep, step,
):
    count, _, rows = in_ref.shape
    frames = count * rows
    length = len_ref[0]
    scale = HDIM ** (-0.5)
    factor = scale * math.log2(math.e)
    half = frames // 2
    steps = frames // step
    blocks = frames // block

    @pl.when(late_ref[0] == 0)
    def _():
        cp = pltpu.make_async_copy(whole_hbm, in_ref, sems.at[0])
        cp.start()
        cp.wait()

    @pl.when(late_ref[0] != 0)
    def _():
        first = pltpu.make_async_copy(part_hbm, in_ref.at[:, : 3 * HDIM], sems.at[0])
        second = pltpu.make_async_copy(d_hbm, in_ref.at[:, 3 * HDIM :], sems.at[1])
        first.start()
        second.start()
        first.wait()
        second.wait()

    for s in range(count):
        at = slice(s * rows, (s + 1) * rows)
        qt_scr[:, at] = in_ref[s, 0:HDIM, :]
        kvt = in_ref[s, HDIM : 3 * HDIM, :]
        kvt_scr[:, at] = kvt
        kv_scr[at, :] = kvt.T
        dt_scr[:, at] = in_ref[s, 3 * HDIM :, :]
    acc_scr[...] = jnp.zeros_like(acc_scr)
    zero = jnp.zeros((HDIM, block), BF)
    none = jnp.zeros((HDIM, block), F32)

    def query(b):
        return jnp.concatenate([qt_scr[:, b * block : (b + 1) * block], zero], axis=0)

    def scores(b):
        qt = query(b)
        top = None
        for i in range(frames // sstep):
            keys = slice(i * sstep, (i + 1) * sstep)
            s = jnp.dot(kv_scr[keys, :], qt, preferred_element_type=F32)
            if (i + 1) * sstep > half:
                pos = i * sstep + lax.broadcasted_iota(jnp.int32, (sstep, block), 0)
                s = jnp.where(pos < length, s, -1e30)
            s_scr[b % 2, keys, :] = s
            part = jnp.max(s.reshape(sstep // 8, 8, block), axis=0)
            top = part if top is None else jnp.maximum(top, part)
        return jnp.max(top, axis=0, keepdims=True)

    def forward(b, i, top, total, out):
        keys = slice(i * step, (i + 1) * step)
        e = jnp.exp2((s_scr[b % 2, keys, :] - top) * factor)
        s_scr[b % 2, keys, :] = e
        eb = e.astype(BF)
        e_scr[b % 2, keys, :] = eb
        total = total + jnp.sum(e.reshape(step // 8, 8, block), axis=0)
        return total, out + jnp.dot(kvt_scr[HDIM:, keys], eb, preferred_element_type=F32)

    def between(b, total, out):
        inv = 1.0 / jnp.sum(total, axis=0, keepdims=True)
        out = out * inv
        dt = dt_scr[:, b * block : (b + 1) * block].astype(F32) * inv
        delta = jnp.sum(dt * out, axis=0, keepdims=True)
        return out, delta, jnp.concatenate([zero, dt.astype(BF)], axis=0)

    def backward(b, i, q0, d0, dt, delta, gq):
        keys = slice(i * step, (i + 1) * step)
        dp = jnp.dot(kv_scr[keys, :], dt, preferred_element_type=F32)
        ds = (s_scr[b % 2, keys, :] * (dp - delta)).astype(BF)
        acc_scr[keys, :] += jnp.dot(ds, q0, preferred_element_type=F32) + jnp.dot(
            e_scr[b % 2, keys, :], d0, preferred_element_type=F32
        )
        return gq + jnp.dot(kvt_scr[:HDIM, keys], ds, preferred_element_type=F32)

    state = None
    for b in range(blocks + 1):
        total, ahead, gq = jnp.zeros((8, block), F32), none, none
        if b < blocks:
            top = scores(b)
        if b > 0:
            out, delta, dt = state
            q0, d0 = query(b - 1).T, dt.T
        for i in range(steps):
            if b < blocks:
                total, ahead = forward(b, i, top, total, ahead)
            if b > 0:
                gq = backward(b - 1, i, q0, d0, dt, delta, gq)
        if b < blocks:
            state = between(b, total, ahead)
        if b > 0:
            gq = (gq * scale).astype(BF)
            out = out.astype(BF)
            for n in range(block // rows):
                at = slice(n * rows, (n + 1) * rows)
                dest = (b - 1) * (block // rows) + n
                out_ref[dest, 0:HDIM, :] = gq[:, at]
                out_ref[dest, 3 * HDIM : 4 * HDIM, :] = out[:, at]
    row = lax.broadcasted_iota(jnp.int32, (2 * HDIM, rows), 0)
    fix = jnp.where(row < HDIM, scale, 1.0)
    for s in range(count):
        acc = acc_scr[s * rows : (s + 1) * rows, :]
        out_ref[s, HDIM : 3 * HDIM, :] = (acc.T * fix).astype(BF)


def back_kernel(
    in_ref, wq_ref, wk_ref, wv_ref, mixed_ref, rstd_ref, gain_ref, gm_ref
):
    rows, width = mixed_ref.shape
    nt = (((1,), (1,)), ((), ()))
    grad = None
    for i, w_ref in enumerate((wq_ref, wk_ref, wv_ref)):
        feats = in_ref[:, i * HDIM : (i + 1) * HDIM, :].reshape(HEADS * HDIM, rows).T
        part = lax.dot_general(feats, w_ref[...], nt, preferred_element_type=F32)
        grad = part if grad is None else grad + part
    scaled = grad * gain_ref[...]
    mixed = mixed_ref[...]
    rstd = rstd_ref[:, 0:1]
    mean = jnp.sum(scaled * mixed, axis=-1, keepdims=True) / width
    gm = rstd * scaled - mixed * (rstd * rstd * rstd * mean)
    gm_ref[...] = gm


def taps_kernel(
    len_ref, first_ref, half_ref, x_ref, near_ref, far_ref, gm_ref, keep_ref, give_ref, edge_ref
):
    rows, width = x_ref.shape
    first = first_ref[0]
    odd = lax.rem(first // rows, 2) == 1
    live = live_rows(first, rows, len_ref[0])
    count = width // 2 // LANES

    def terms(lanes):
        low, high = ends(first, near_ref, far_ref, lanes, rows, len_ref[0])
        padded = jnp.concatenate([low, x_ref[:, lanes].astype(F32) * live, high], axis=0)
        gm = gm_ref[:, lanes]
        result = [None] * (KSIZE + 1)
        for r in range(8):
            fill = [jnp.zeros((r, LANES), F32)] if r else []
            ext = jnp.concatenate(fill + [gm, jnp.zeros((8 - r, LANES), F32)], axis=0)
            for a in range(4):
                o = 8 * a + r
                if o == 0:
                    continue
                prod = ext * padded[8 * a : 8 * a + rows + 8]
                result[o - 1] = jnp.sum(prod, axis=0, keepdims=True)
        result[KSIZE] = jnp.zeros((1, LANES), F32)
        return jnp.concatenate(result, axis=0)

    def step(c, _):
        keep_ref[:, chunk(c)] = terms(chunk(c + half_ref[0] * count))
        give_ref[: KSIZE + 1, chunk(c)] = terms(chunk(c + (1 - half_ref[0]) * count)).astype(BF)
        for n in range(2):
            lanes = chunk(c + n * count)
            head = gm_ref[:PAD, lanes]
            tail = gm_ref[rows - PAD :, lanes]
            at = n * PAD
            give_ref[KSIZE + 1 + at : KSIZE + 1 + at + PAD, chunk(c)] = jnp.where(
                odd, head, tail
            ).astype(BF)
            edge_ref[at : at + PAD, chunk(c)] = jnp.where(odd, tail, head).astype(BF)
        return 0

    lax.fori_loop(0, count, step, 0)


def own_kernel(len_ref, first_ref, in_ref, gm_ref, taps_ref, attn_ref, own_ref):
    rows, width = gm_ref.shape
    live = live_rows(first_ref[0], rows, len_ref[0])
    zero = jnp.zeros((PAD, LANES), F32)

    def step(c, _):
        lanes = chunk(c)
        gm = gm_ref[:, lanes]
        padded = jnp.concatenate([zero, gm, zero], axis=0)
        own_ref[:, lanes] = gm + live * conv_chunk(padded, taps_ref, lanes, rows, True)
        return 0

    lax.fori_loop(0, width // LANES, step, 0)
    out = in_ref[:, 3 * HDIM : 4 * HDIM, :].reshape(HEADS * HDIM, rows).T
    attn_ref[...] = (out.astype(F32) * live[:, 0:1]).astype(BF)


def final_kernel(
    len_ref, first_ref, own_ref, near_ref, far_ref, taps_ref, gi_ref, *, frames,
):
    rows, width = own_ref.shape
    first = first_ref[0]
    live = live_rows(first, rows, len_ref[0])
    count = width // 2 // LANES

    def step(c, _):
        for n in range(2):
            lanes = chunk(c + n * count)
            at = KSIZE + 1 + n * PAD
            low, high = ends(
                first, near_ref.at[at : at + PAD], far_ref.at[at : at + PAD], chunk(c), rows, frames
            )
            top, end = edge_convs(low, high, taps_ref, lanes, True)
            gi_ref[:PAD, lanes] = (own_ref[:PAD, lanes] + live[:PAD] * top).astype(BF)
            gi_ref[PAD : rows - PAD, lanes] = own_ref[PAD : rows - PAD, lanes].astype(BF)
            gi_ref[rows - PAD :, lanes] = (
                own_ref[rows - PAD :, lanes] + live[rows - PAD :] * end
            ).astype(BF)
        return 0

    lax.fori_loop(0, count, step, 0)


def params(mib):
    return pltpu.CompilerParams(vmem_limit_bytes=mib << 20)


def cost(us):
    return pl.CostEstimate(flops=int(us * 1.1e9), bytes_accessed=1024, transcendentals=0)


def local(inputs, lengths, kernel, gain, q_weight, k_weight, v_weight, grad_attn):
    rows, width = inputs.shape
    count = lax.axis_size("seq")
    frames = rows * count
    feats = HEADS * HDIM
    sds = jax.ShapeDtypeStruct
    here = lax.axis_index("seq")
    odd = lax.rem(here, 2)
    first = (here * rows).astype(jnp.int32).reshape(1)
    gain = gain.reshape(1, width)

    def peer(mine, move):
        return lax.ppermute(mine, "seq", [(i, move(i)) for i in range(count)])

    def near(mine):
        return peer(mine, lambda i: i ^ 1)

    def far(mine):
        return peer(mine, lambda i: (i + 1 if i % 2 else i - 1) % count)

    a2a = functools.partial(
        lax.all_to_all, axis_name="seq", split_axis=0, concat_axis=0, tiled=True
    )
    slices = (
        lax.dynamic_slice_in_dim(inputs, odd * (rows - PAD), PAD),
        lax.dynamic_slice_in_dim(inputs, (1 - odd) * (rows - PAD), PAD),
    )
    for_far, for_near, after = lax.optimization_barrier(slices + (first,))
    x_far = far(for_far)
    x_near = near(for_near)

    def in_hbm(array):
        return pltpu.with_memory_space_constraint(array, pltpu.HBM)

    late = lax.rem(lax.axis_index("dp"), 4) >= 2
    douts = pl.pallas_call(
        dout_kernel,
        name="dout",
        out_shape=sds((feats, rows), BF),
        in_specs=[SMEM, SMEM, VMEM],
        out_specs=VMEM,
        compiler_params=params(4),
        cost_estimate=cost(1),
    )(lengths, after, in_hbm(grad_attn)).reshape(HEADS, HDIM, rows)
    douts = lax.cond(late, a2a, lambda d: d, douts)
    ready, douts = lax.optimization_barrier((first, douts))
    own, weights = pl.pallas_call(
        early_kernel,
        name="early",
        out_shape=(
            pltpu.VMEM((rows, width), F32),
            pltpu.VMEM((3, width, feats), BF),
        ),
        in_specs=[SMEM, SMEM] + [HBM] * 5,
        out_specs=(VMEM,) * 2,
        scratch_shapes=[
            pltpu.VMEM((rows, width), BF),
            pltpu.VMEM((KSIZE, width), F32),
            pltpu.SemaphoreType.DMA((5,)),
        ],
        compiler_params=params(16),
        cost_estimate=cost(6),
    )(lengths, ready, *(in_hbm(a) for a in (inputs, kernel, q_weight, k_weight, v_weight)))
    send, send_all, mixed, rstd = pl.pallas_call(
        pre_kernel,
        name="pre",
        out_shape=(
            sds((HEADS, 3 * HDIM, rows), BF),
            sds((HEADS, 4 * HDIM, rows), BF),
            sds((rows, width), F32),
            sds((rows, LANES), F32),
        ),
        in_specs=[SMEM, SMEM] + [VMEM] * 7,
        out_specs=(VMEM,) * 4,
        compiler_params=params(16),
        cost_estimate=cost(3),
    )(lengths, first, own, x_near, x_far, kernel, gain, weights, douts)

    block, sstep, step = 512, 1024, 512

    part, whole = lax.cond(
        late,
        lambda part, whole: lax.optimization_barrier((a2a(part), whole)),
        lambda part, whole: (part, a2a(whole)),
        send, send_all,
    )
    heads_out = pl.pallas_call(
        functools.partial(attn_kernel, block=block, sstep=sstep, step=step),
        name="attn",
        out_shape=sds((HEADS, 4 * HDIM, rows), BF),
        in_specs=[SMEM, SMEM] + [ANY] * 3,
        out_specs=VMEM,
        scratch_shapes=[
            pltpu.VMEM((HEADS, 4 * HDIM, rows), BF),
            pltpu.VMEM((HDIM, frames), BF),
            pltpu.VMEM((HDIM, frames), BF),
            pltpu.VMEM((2 * HDIM, frames), BF),
            pltpu.VMEM((frames, 2 * HDIM), BF),
            pltpu.VMEM((2, frames, block), F32),
            pltpu.VMEM((2, frames, block), BF),
            pltpu.VMEM((frames, 2 * HDIM), F32),
            pltpu.SemaphoreType.DMA((2,)),
        ],
        compiler_params=params(32),
        cost_estimate=cost(15),
    )(lengths, late.astype(jnp.int32).reshape(1), part, whole, douts)
    grads = a2a(heads_out)

    gm = pl.pallas_call(
        back_kernel,
        name="back",
        out_shape=sds((rows, width), F32),
        in_specs=[VMEM] * 7,
        out_specs=VMEM,
        compiler_params=params(16),
        cost_estimate=cost(4),
    )(grads, q_weight, k_weight, v_weight, mixed, rstd, gain)
    here, gm = lax.optimization_barrier((here, gm))
    half = ((here ^ (here >> 1)) & 1).astype(jnp.int32)
    keep, give, edge = pl.pallas_call(
        taps_kernel,
        name="taps",
        out_shape=(
            sds((KSIZE + 1, width // 2), F32),
            sds((KSIZE + 1 + 2 * PAD, width // 2), BF),
            sds((2 * PAD, width // 2), BF),
        ),
        in_specs=[SMEM] * 3 + [VMEM] * 4,
        out_specs=(VMEM,) * 3,
        compiler_params=params(16),
        cost_estimate=cost(3),
    )(lengths, first, half.reshape(1), inputs, x_near, x_far, gm)

    got = near(give)
    mine = (keep + got[: KSIZE + 1].astype(F32)).astype(BF)
    one, two, three = (peer(mine, lambda i: i ^ bits).astype(F32) for bits in (4, 8, 12))
    mine = ((mine.astype(F32) + one) + (two + three)).astype(BF)
    last = far(jnp.concatenate([mine, edge], axis=0))
    attn, own_gi = pl.pallas_call(
        own_kernel,
        name="own",
        out_shape=(sds((rows, feats), BF), sds((rows, width), F32)),
        in_specs=[SMEM, SMEM] + [VMEM] * 3,
        out_specs=(VMEM,) * 2,
        compiler_params=params(16),
        cost_estimate=cost(3),
    )(lengths, first, grads, gm, kernel)
    mine = (mine.astype(F32) + last[: KSIZE + 1].astype(F32)).astype(BF)
    other = near(mine)
    grad_input = pl.pallas_call(
        functools.partial(final_kernel, frames=frames),
        name="final",
        out_shape=sds((rows, width), BF),
        in_specs=[SMEM, SMEM] + [VMEM] * 4,
        out_specs=VMEM,
        compiler_params=params(16),
        cost_estimate=cost(1),
    )(lengths, first, own_gi, got, last, kernel)
    left = jnp.where(half == 0, mine, other)
    right = jnp.where(half == 0, other, mine)
    grad_kernel = jnp.concatenate([left, right], axis=1)[:KSIZE].astype(F32)
    return (attn, grad_input, grad_kernel)


def solution(mesh):
    placed = (P(("dp", "seq"), None), P("dp"), P(), P(), P(), P(), P(), P(("dp", "seq"), None))
    return jax.shard_map(
        local,
        mesh=mesh,
        in_specs=placed,
        out_specs=(P(("dp", "seq"), None), P(("dp", "seq"), None), P("dp", None)),
        check_vma=False,
    )
```

```python
import functools
import math

import jax
import jax.numpy as jnp
from jax import lax
from jax.experimental import pallas as pl
from jax.experimental.pallas import tpu as pltpu
from jax.sharding import PartitionSpec as P

HEADS = 16
HDIM = 64
KSIZE = 31
PAD = 16
LANES = 128
BF = jnp.bfloat16
F32 = jnp.float32
VMEM = pl.BlockSpec(memory_space=pltpu.VMEM)
SMEM = pl.BlockSpec(memory_space=pltpu.SMEM)
HBM = pl.BlockSpec(memory_space=pltpu.HBM)
ANY = pl.BlockSpec(memory_space=pl.ANY)


def live_rows(first, rows, length):
    pos = first + lax.broadcasted_iota(jnp.int32, (rows, LANES), 0)
    return ((pos >= 0) & (pos < length)).astype(F32)


def ends(first, near_ref, far_ref, lanes, rows, length):
    odd = lax.rem(first // rows, 2) == 1
    near = near_ref[:, lanes].astype(F32)
    far = far_ref[:, lanes].astype(F32)
    low = jnp.where(odd, near, far) * live_rows(first - PAD, PAD, length)
    high = jnp.where(odd, far, near) * live_rows(first + rows, PAD, length)
    return low, high


def conv_chunk(padded, taps_ref, lanes, rows, reverse):
    total = None
    for r in range(8):
        acc = None
        for a in range(4):
            o = 8 * a + r
            if o == 0:
                continue
            j = KSIZE - o if reverse else o - 1
            term = taps_ref[j : j + 1, lanes] * padded[8 * a : 8 * a + rows + 8]
            acc = term if acc is None else acc + term
        part = acc[r : r + rows]
        total = part if total is None else total + part
    return total


def chunk(c):
    return pl.ds(pl.multiple_of(c * LANES, LANES), LANES)


def dout_kernel(len_ref, first_ref, g_ref, out_ref):
    live = live_rows(first_ref[0], g_ref.shape[0], len_ref[0])
    out_ref[...] = (g_ref[...].astype(F32) * live[:, 0:1]).T.astype(BF)


def early_kernel(
    len_ref, first_ref, x_hbm, taps_hbm, wq_ref, wk_ref, wv_ref,
    conv_ref, w_ref, x_ref, taps_ref, sems,
):
    rows, width = x_ref.shape
    moves = ((x_hbm, x_ref), (taps_hbm, taps_ref))
    moves += tuple((w, w_ref.at[i]) for i, w in enumerate((wq_ref, wk_ref, wv_ref)))
    copies = [pltpu.make_async_copy(*m, sems.at[i]) for i, m in enumerate(moves)]
    for cp in copies:
        cp.start()
    live = live_rows(first_ref[0], rows, len_ref[0])
    zero = jnp.zeros((PAD, LANES), F32)
    for cp in copies[:2]:
        cp.wait()

    def conv_step(c, _):
        lanes = chunk(c)
        x = x_ref[:, lanes].astype(F32)
        padded = jnp.concatenate([zero, x * live, zero], axis=0)
        conv_ref[:, lanes] = x + conv_chunk(padded, taps_ref, lanes, rows, False)
        return 0

    lax.fori_loop(0, width // LANES, conv_step, 0)
    for cp in copies[2:]:
        cp.wait()


def edge_convs(low, high, taps_ref, lanes, reverse):
    zero = jnp.zeros((2 * PAD, LANES), F32)
    top = conv_chunk(jnp.concatenate([low, zero], axis=0), taps_ref, lanes, PAD, reverse)
    end = conv_chunk(jnp.concatenate([zero, high], axis=0), taps_ref, lanes, PAD, reverse)
    return top, end


def pre_kernel(
    len_ref, first_ref, conv_ref, near_ref, far_ref, taps_ref, gain_ref, w_ref, d_ref,
    send_ref, all_ref, mixed_ref, rstd_ref,
):
    rows, width = conv_ref.shape

    def conv_step(c, sq):
        lanes = chunk(c)
        low, high = ends(first_ref[0], near_ref, far_ref, lanes, rows, len_ref[0])
        top, end = edge_convs(low, high, taps_ref, lanes, False)
        mixed = jnp.concatenate(
            [
                conv_ref[:PAD, lanes] + top,
                conv_ref[PAD : rows - PAD, lanes],
                conv_ref[rows - PAD :, lanes] + end,
            ],
            axis=0,
        )
        mixed_ref[:, lanes] = mixed
        return sq + mixed * mixed

    sq = lax.fori_loop(0, width // LANES, conv_step, jnp.zeros((rows, LANES), F32))
    rstd = lax.rsqrt(jnp.sum(sq, axis=-1, keepdims=True) / width + 1e-05)
    rstd_ref[...] = jnp.broadcast_to(rstd, (rows, LANES))
    normed = (mixed_ref[...] * rstd * gain_ref[...]).astype(BF)
    for i in range(3):
        heads = jnp.dot(normed, w_ref[i], preferred_element_type=F32)
        heads = heads.T.astype(BF).reshape(HEADS, HDIM, rows)
        send_ref[:, i * HDIM : (i + 1) * HDIM, :] = heads
        all_ref[:, i * HDIM : (i + 1) * HDIM, :] = heads
    all_ref[:, 3 * HDIM :, :] = d_ref[...]


def attn_kernel(
    len_ref, late_ref, part_hbm, whole_hbm, d_hbm, out_ref, in_ref, qt_scr, dt_scr, kvt_scr, kv_scr,
    s_scr, e_scr, acc_scr, top_scr, sems, *, block, sstep, step,
):
    count, _, rows = in_ref.shape
    frames = count * rows
    length = len_ref[0]
    scale = HDIM ** (-0.5)
    factor = scale * math.log2(math.e)
    half = frames // 2
    steps = frames // step
    blocks = frames // block

    @pl.when(late_ref[0] == 0)
    def _():
        cp = pltpu.make_async_copy(whole_hbm, in_ref, sems.at[0])
        cp.start()
        cp.wait()

    @pl.when(late_ref[0] != 0)
    def _():
        first = pltpu.make_async_copy(part_hbm, in_ref.at[:, : 3 * HDIM], sems.at[0])
        second = pltpu.make_async_copy(d_hbm, in_ref.at[:, 3 * HDIM :], sems.at[1])
        first.start()
        second.start()
        first.wait()
        second.wait()

    for s in range(count):
        at = slice(s * rows, (s + 1) * rows)
        qt_scr[:, at] = in_ref[s, 0:HDIM, :]
        kvt = in_ref[s, HDIM : 3 * HDIM, :]
        kvt_scr[:, at] = kvt
        kv_scr[at, :] = kvt.T
        dt_scr[:, at] = in_ref[s, 3 * HDIM :, :]
    acc_scr[...] = jnp.zeros_like(acc_scr)
    zero = jnp.zeros((HDIM, block), BF)

    def masked_scores(first, rows, qt):
        s = jnp.dot(kv_scr[pl.ds(first, rows), :], qt, preferred_element_type=F32)
        pos = first + lax.broadcasted_iota(jnp.int32, (rows, block), 0)
        return jnp.where(pos < length, s, -1e30)

    def squares(ref, rows):
        return jnp.sum(jnp.square(ref[rows, :].astype(F32)), axis=0, keepdims=True)

    longest = jnp.max(squares(kvt_scr, slice(0, HDIM)), axis=-1, keepdims=True)
    bound = jnp.sqrt(squares(qt_scr, slice(0, HDIM)) * longest)
    top_scr[...] = bound
    in_range = jnp.max(bound) * (2 * factor) < 100.0

    @pl.when(jnp.logical_not(in_range))
    def _():
        def one(b, _):
            cols = pl.ds(pl.multiple_of(b * block, block), block)
            qt = jnp.concatenate([qt_scr[:, cols], zero], axis=0)

            def more(i, top):
                s = masked_scores(pl.multiple_of(i * rows, rows), rows, qt)
                return jnp.maximum(top, jnp.max(s, axis=0, keepdims=True))

            top = jnp.full((1, block), -1e30, F32)
            top_scr[:, cols] = lax.fori_loop(0, frames // rows, more, top)
            return 0

        lax.fori_loop(0, blocks, one, 0)

    none = jnp.zeros((HDIM, block), F32)

    def query(b):
        return jnp.concatenate([qt_scr[:, b * block : (b + 1) * block], zero], axis=0)

    def scores(b):
        qt = query(b)
        for i in range(frames // sstep):
            keys = slice(i * sstep, (i + 1) * sstep)
            if (i + 1) * sstep > half:
                s_scr[b % 2, keys, :] = masked_scores(i * sstep, sstep, qt)
            else:
                s_scr[b % 2, keys, :] = jnp.dot(kv_scr[keys, :], qt, preferred_element_type=F32)
        return top_scr[:, b * block : (b + 1) * block]

    def forward(b, i, top, total, out):
        keys = slice(i * step, (i + 1) * step)
        e = jnp.exp2((s_scr[b % 2, keys, :] - top) * factor)
        s_scr[b % 2, keys, :] = e
        eb = e.astype(BF)
        e_scr[b % 2, keys, :] = eb
        total = total + jnp.sum(e.reshape(step // 8, 8, block), axis=0)
        return total, out + jnp.dot(kvt_scr[HDIM:, keys], eb, preferred_element_type=F32)

    def between(b, total, out):
        inv = 1.0 / jnp.sum(total, axis=0, keepdims=True)
        out = out * inv
        dt = dt_scr[:, b * block : (b + 1) * block].astype(F32) * inv
        delta = jnp.sum(dt * out, axis=0, keepdims=True)
        return out, delta, jnp.concatenate([zero, dt.astype(BF)], axis=0)

    def backward(b, i, q0, d0, dt, delta, gq):
        keys = slice(i * step, (i + 1) * step)
        dp = jnp.dot(kv_scr[keys, :], dt, preferred_element_type=F32)
        ds = (s_scr[b % 2, keys, :] * (dp - delta)).astype(BF)
        acc_scr[keys, :] += jnp.dot(ds, q0, preferred_element_type=F32) + jnp.dot(
            e_scr[b % 2, keys, :], d0, preferred_element_type=F32
        )
        return gq + jnp.dot(kvt_scr[:HDIM, keys], ds, preferred_element_type=F32)

    state = None
    for b in range(blocks + 1):
        total, ahead, gq = jnp.zeros((8, block), F32), none, none
        if b < blocks:
            top = scores(b)
        if b > 0:
            out, delta, dt = state
            q0, d0 = query(b - 1).T, dt.T
        for i in range(steps):
            if b < blocks:
                total, ahead = forward(b, i, top, total, ahead)
            if b > 0:
                gq = backward(b - 1, i, q0, d0, dt, delta, gq)
        if b < blocks:
            state = between(b, total, ahead)
        if b > 0:
            gq = (gq * scale).astype(BF)
            out = out.astype(BF)
            for n in range(block // rows):
                at = slice(n * rows, (n + 1) * rows)
                dest = (b - 1) * (block // rows) + n
                out_ref[dest, 0:HDIM, :] = gq[:, at]
                out_ref[dest, 3 * HDIM : 4 * HDIM, :] = out[:, at]
    row = lax.broadcasted_iota(jnp.int32, (2 * HDIM, rows), 0)
    fix = jnp.where(row < HDIM, scale, 1.0)
    for s in range(count):
        acc = acc_scr[s * rows : (s + 1) * rows, :]
        out_ref[s, HDIM : 3 * HDIM, :] = (acc.T * fix).astype(BF)


def back_kernel(
    in_ref, wq_ref, wk_ref, wv_ref, mixed_ref, rstd_ref, gain_ref, gm_ref
):
    rows, width = mixed_ref.shape
    nt = (((1,), (1,)), ((), ()))
    grad = None
    for i, w_ref in enumerate((wq_ref, wk_ref, wv_ref)):
        feats = in_ref[:, i * HDIM : (i + 1) * HDIM, :].reshape(HEADS * HDIM, rows).T
        part = lax.dot_general(feats, w_ref[...], nt, preferred_element_type=F32)
        grad = part if grad is None else grad + part
    scaled = grad * gain_ref[...]
    mixed = mixed_ref[...]
    rstd = rstd_ref[:, 0:1]
    mean = jnp.sum(scaled * mixed, axis=-1, keepdims=True) / width
    gm = rstd * scaled - mixed * (rstd * rstd * rstd * mean)
    gm_ref[...] = gm


def taps_terms(len_ref, first_ref, x_ref, near_ref, far_ref, gm_ref, lanes):
    rows = x_ref.shape[0]
    first = first_ref[0]
    low, high = ends(first, near_ref, far_ref, lanes, rows, len_ref[0])
    live = live_rows(first, rows, len_ref[0])
    padded = jnp.concatenate([low, x_ref[:, lanes].astype(F32) * live, high], axis=0)
    gm = gm_ref[:, lanes]
    result = [None] * (KSIZE + 1)
    for r in range(8):
        fill = [jnp.zeros((r, LANES), F32)] if r else []
        ext = jnp.concatenate(fill + [gm, jnp.zeros((8 - r, LANES), F32)], axis=0)
        for a in range(4):
            o = 8 * a + r
            if o == 0:
                continue
            prod = ext * padded[8 * a : 8 * a + rows + 8]
            result[o - 1] = jnp.sum(prod, axis=0, keepdims=True)
    result[KSIZE] = jnp.zeros((1, LANES), F32)
    return jnp.concatenate(result, axis=0)


def give_kernel(
    len_ref, first_ref, half_ref, x_ref, near_ref, far_ref, gm_ref, give_ref, edge_ref
):
    rows, width = x_ref.shape
    odd = lax.rem(first_ref[0] // rows, 2) == 1
    count = width // 2 // LANES

    def step(c, _):
        lanes = chunk(c + (1 - half_ref[0]) * count)
        give_ref[: KSIZE + 1, chunk(c)] = taps_terms(
            len_ref, first_ref, x_ref, near_ref, far_ref, gm_ref, lanes
        ).astype(BF)
        for n in range(2):
            lanes = chunk(c + n * count)
            head = gm_ref[:PAD, lanes]
            tail = gm_ref[rows - PAD :, lanes]
            at = n * PAD
            give_ref[KSIZE + 1 + at : KSIZE + 1 + at + PAD, chunk(c)] = jnp.where(
                odd, head, tail
            ).astype(BF)
            edge_ref[at : at + PAD, chunk(c)] = jnp.where(odd, tail, head).astype(BF)
        return 0

    lax.fori_loop(0, count, step, 0)


def keep_kernel(len_ref, first_ref, half_ref, x_ref, near_ref, far_ref, gm_ref, keep_ref):
    count = x_ref.shape[1] // 2 // LANES

    def step(c, _):
        keep_ref[:, chunk(c)] = taps_terms(
            len_ref, first_ref, x_ref, near_ref, far_ref, gm_ref, chunk(c + half_ref[0] * count)
        )
        return 0

    lax.fori_loop(0, count, step, 0)


def join_kernel(mine_ref, one_ref, two_ref, three_ref, edge_ref, out_ref):
    mine, one, two, three = (r[...].astype(F32) for r in (mine_ref, one_ref, two_ref, three_ref))
    out_ref[: KSIZE + 1] = ((mine + one) + (two + three)).astype(BF)
    out_ref[KSIZE + 1 :] = edge_ref[...]


def own_kernel(len_ref, first_ref, in_ref, gm_ref, taps_ref, attn_ref, own_ref):
    rows, width = gm_ref.shape
    live = live_rows(first_ref[0], rows, len_ref[0])
    zero = jnp.zeros((PAD, LANES), F32)

    def step(c, _):
        lanes = chunk(c)
        gm = gm_ref[:, lanes]
        padded = jnp.concatenate([zero, gm, zero], axis=0)
        own_ref[:, lanes] = gm + live * conv_chunk(padded, taps_ref, lanes, rows, True)
        return 0

    lax.fori_loop(0, width // LANES, step, 0)
    out = in_ref[:, 3 * HDIM : 4 * HDIM, :].reshape(HEADS * HDIM, rows).T
    attn_ref[...] = (out.astype(F32) * live[:, 0:1]).astype(BF)


def final_kernel(
    len_ref, first_ref, own_ref, near_ref, far_ref, taps_ref, gi_ref, *, frames,
):
    rows, width = own_ref.shape
    first = first_ref[0]
    live = live_rows(first, rows, len_ref[0])
    count = width // 2 // LANES

    def step(c, _):
        for n in range(2):
            lanes = chunk(c + n * count)
            at = KSIZE + 1 + n * PAD
            low, high = ends(
                first, near_ref.at[at : at + PAD], far_ref.at[at : at + PAD], chunk(c), rows, frames
            )
            top, end = edge_convs(low, high, taps_ref, lanes, True)
            gi_ref[:PAD, lanes] = (own_ref[:PAD, lanes] + live[:PAD] * top).astype(BF)
            gi_ref[PAD : rows - PAD, lanes] = own_ref[PAD : rows - PAD, lanes].astype(BF)
            gi_ref[rows - PAD :, lanes] = (
                own_ref[rows - PAD :, lanes] + live[rows - PAD :] * end
            ).astype(BF)
        return 0

    lax.fori_loop(0, count, step, 0)


def params(mib):
    return pltpu.CompilerParams(vmem_limit_bytes=mib << 20)


def cost(us):
    return pl.CostEstimate(flops=int(us * 1.1e9), bytes_accessed=1024, transcendentals=0)


def local(inputs, lengths, kernel, gain, q_weight, k_weight, v_weight, grad_attn):
    rows, width = inputs.shape
    count = lax.axis_size("seq")
    frames = rows * count
    feats = HEADS * HDIM
    sds = jax.ShapeDtypeStruct
    here = lax.axis_index("seq")
    odd = lax.rem(here, 2)
    first = (here * rows).astype(jnp.int32).reshape(1)
    gain = gain.reshape(1, width)

    def peer(mine, move):
        return lax.ppermute(mine, "seq", [(i, move(i)) for i in range(count)])

    def near(mine):
        return peer(mine, lambda i: i ^ 1)

    def far(mine):
        return peer(mine, lambda i: (i + 1 if i % 2 else i - 1) % count)

    a2a = functools.partial(
        lax.all_to_all, axis_name="seq", split_axis=0, concat_axis=0, tiled=True
    )
    slices = (
        lax.dynamic_slice_in_dim(inputs, odd * (rows - PAD), PAD),
        lax.dynamic_slice_in_dim(inputs, (1 - odd) * (rows - PAD), PAD),
    )
    for_far, for_near, after = lax.optimization_barrier(slices + (first,))
    x_far = far(for_far)
    x_near = near(for_near)

    def in_hbm(array):
        return pltpu.with_memory_space_constraint(array, pltpu.HBM)

    late = lax.rem(lax.axis_index("dp"), 4) >= 2
    douts = pl.pallas_call(
        dout_kernel,
        name="dout",
        out_shape=sds((feats, rows), BF),
        in_specs=[SMEM, SMEM, VMEM],
        out_specs=VMEM,
        compiler_params=params(4),
        cost_estimate=cost(1),
    )(lengths, after, in_hbm(grad_attn)).reshape(HEADS, HDIM, rows)
    douts = lax.cond(late, a2a, lambda d: d, douts)
    ready, douts = lax.optimization_barrier((first, douts))
    own, weights = pl.pallas_call(
        early_kernel,
        name="early",
        out_shape=(
            pltpu.VMEM((rows, width), F32),
            pltpu.VMEM((3, width, feats), BF),
        ),
        in_specs=[SMEM, SMEM] + [HBM] * 5,
        out_specs=(VMEM,) * 2,
        scratch_shapes=[
            pltpu.VMEM((rows, width), BF),
            pltpu.VMEM((KSIZE, width), F32),
            pltpu.SemaphoreType.DMA((5,)),
        ],
        compiler_params=params(16),
        cost_estimate=cost(6),
    )(lengths, ready, *(in_hbm(a) for a in (inputs, kernel, q_weight, k_weight, v_weight)))
    send, send_all, mixed, rstd = pl.pallas_call(
        pre_kernel,
        name="pre",
        out_shape=(
            sds((HEADS, 3 * HDIM, rows), BF),
            sds((HEADS, 4 * HDIM, rows), BF),
            sds((rows, width), F32),
            sds((rows, LANES), F32),
        ),
        in_specs=[SMEM, SMEM] + [VMEM] * 7,
        out_specs=(VMEM,) * 4,
        compiler_params=params(16),
        cost_estimate=cost(3),
    )(lengths, first, own, x_near, x_far, kernel, gain, weights, douts)

    block, sstep, step = 512, 1024, 512

    part, whole = lax.cond(
        late,
        lambda part, whole: lax.optimization_barrier((a2a(part), whole)),
        lambda part, whole: (part, a2a(whole)),
        send, send_all,
    )
    heads_out = pl.pallas_call(
        functools.partial(attn_kernel, block=block, sstep=sstep, step=step),
        name="attn",
        out_shape=sds((HEADS, 4 * HDIM, rows), BF),
        in_specs=[SMEM, SMEM] + [ANY] * 3,
        out_specs=VMEM,
        scratch_shapes=[
            pltpu.VMEM((HEADS, 4 * HDIM, rows), BF),
            pltpu.VMEM((HDIM, frames), BF),
            pltpu.VMEM((HDIM, frames), BF),
            pltpu.VMEM((2 * HDIM, frames), BF),
            pltpu.VMEM((frames, 2 * HDIM), BF),
            pltpu.VMEM((2, frames, block), F32),
            pltpu.VMEM((2, frames, block), BF),
            pltpu.VMEM((frames, 2 * HDIM), F32),
            pltpu.VMEM((1, frames), F32),
            pltpu.SemaphoreType.DMA((2,)),
        ],
        compiler_params=params(32),
        cost_estimate=cost(15),
    )(lengths, late.astype(jnp.int32).reshape(1), part, whole, douts)
    grads = a2a(heads_out)

    gm = pl.pallas_call(
        back_kernel,
        name="back",
        out_shape=sds((rows, width), F32),
        in_specs=[VMEM] * 7,
        out_specs=VMEM,
        compiler_params=params(16),
        cost_estimate=cost(4),
    )(grads, q_weight, k_weight, v_weight, mixed, rstd, gain)
    here, gm = lax.optimization_barrier((here, gm))
    half = ((here ^ (here >> 1)) & 1).astype(jnp.int32)
    given = (lengths, first, half.reshape(1), inputs, x_near, x_far, gm)
    give, edge = pl.pallas_call(
        give_kernel,
        name="give",
        out_shape=(
            sds((KSIZE + 1 + 2 * PAD, width // 2), BF),
            sds((2 * PAD, width // 2), BF),
        ),
        in_specs=[SMEM] * 3 + [VMEM] * 4,
        out_specs=(VMEM,) * 2,
        compiler_params=params(16),
        cost_estimate=cost(2),
    )(*given)
    keep = pl.pallas_call(
        keep_kernel,
        name="keep",
        out_shape=sds((KSIZE + 1, width // 2), F32),
        in_specs=[SMEM] * 3 + [VMEM] * 4,
        out_specs=VMEM,
        compiler_params=params(16),
        cost_estimate=cost(2),
    )(*given)

    got = near(give)
    mine = (keep + got[: KSIZE + 1].astype(F32)).astype(BF)
    parts = [peer(mine, lambda i: i ^ bits) for bits in (4, 8, 12)]
    joined = pl.pallas_call(
        join_kernel,
        name="join",
        out_shape=sds((KSIZE + 1 + 2 * PAD, width // 2), BF),
        in_specs=[VMEM] * 5,
        out_specs=VMEM,
        compiler_params=params(4),
        cost_estimate=cost(1),
    )(mine, *parts, edge)
    last = far(joined)
    attn, own_gi = pl.pallas_call(
        own_kernel,
        name="own",
        out_shape=(sds((rows, feats), BF), sds((rows, width), F32)),
        in_specs=[SMEM, SMEM] + [VMEM] * 3,
        out_specs=(VMEM,) * 2,
        compiler_params=params(16),
        cost_estimate=cost(3),
    )(lengths, first, grads, gm, kernel)
    mine = (joined[: KSIZE + 1].astype(F32) + last[: KSIZE + 1].astype(F32)).astype(BF)
    other = near(mine)
    grad_input = pl.pallas_call(
        functools.partial(final_kernel, frames=frames),
        name="final",
        out_shape=sds((rows, width), BF),
        in_specs=[SMEM, SMEM] + [VMEM] * 4,
        out_specs=VMEM,
        compiler_params=params(16),
        cost_estimate=cost(1),
    )(lengths, first, own_gi, got, last, kernel)
    left = jnp.where(half == 0, mine, other)
    right = jnp.where(half == 0, other, mine)
    grad_kernel = jnp.concatenate([left, right], axis=1)[:KSIZE].astype(F32)
    return (attn, grad_input, grad_kernel)


def solution(mesh):
    placed = (P(("dp", "seq"), None), P("dp"), P(), P(), P(), P(), P(), P(("dp", "seq"), None))
    return jax.shard_map(
        local,
        mesh=mesh,
        in_specs=placed,
        out_specs=(P(("dp", "seq"), None), P(("dp", "seq"), None), P("dp", None)),
        check_vma=False,
    )
```

```python
import functools
import math

import jax
import jax.numpy as jnp
from jax import lax
from jax.experimental import pallas as pl
from jax.experimental.pallas import tpu as pltpu
from jax.sharding import PartitionSpec as P

HEADS = 16
HDIM = 64
KSIZE = 31
PAD = 16
LANES = 128
BF = jnp.bfloat16
F32 = jnp.float32
VMEM = pl.BlockSpec(memory_space=pltpu.VMEM)
SMEM = pl.BlockSpec(memory_space=pltpu.SMEM)
HBM = pl.BlockSpec(memory_space=pltpu.HBM)
ANY = pl.BlockSpec(memory_space=pl.ANY)


def live_rows(first, rows, length):
    pos = first + lax.broadcasted_iota(jnp.int32, (rows, LANES), 0)
    return ((pos >= 0) & (pos < length)).astype(F32)


def ends(first, near_ref, far_ref, lanes, rows, length):
    odd = lax.rem(first // rows, 2) == 1
    near = near_ref[:, lanes].astype(F32)
    far = far_ref[:, lanes].astype(F32)
    low = jnp.where(odd, near, far) * live_rows(first - PAD, PAD, length)
    high = jnp.where(odd, far, near) * live_rows(first + rows, PAD, length)
    return low, high


def conv_chunk(padded, taps_ref, lanes, rows, reverse):
    total = None
    for r in range(8):
        acc = None
        for a in range(4):
            o = 8 * a + r
            if o == 0:
                continue
            j = KSIZE - o if reverse else o - 1
            term = taps_ref[j : j + 1, lanes] * padded[8 * a : 8 * a + rows + 8]
            acc = term if acc is None else acc + term
        part = acc[r : r + rows]
        total = part if total is None else total + part
    return total


def chunk(c):
    return pl.ds(pl.multiple_of(c * LANES, LANES), LANES)


def dout_kernel(len_ref, first_ref, g_ref, out_ref):
    live = live_rows(first_ref[0], g_ref.shape[0], len_ref[0])
    out_ref[...] = (g_ref[...].astype(F32) * live[:, 0:1]).T.astype(BF)


def early_kernel(
    len_ref, first_ref, x_hbm, taps_hbm, wq_ref, wk_ref, wv_ref,
    conv_ref, w_ref, x_ref, taps_ref, sems,
):
    rows, width = x_ref.shape
    moves = ((x_hbm, x_ref), (taps_hbm, taps_ref))
    moves += tuple((w, w_ref.at[i]) for i, w in enumerate((wq_ref, wk_ref, wv_ref)))
    copies = [pltpu.make_async_copy(*m, sems.at[i]) for i, m in enumerate(moves)]
    for cp in copies:
        cp.start()
    live = live_rows(first_ref[0], rows, len_ref[0])
    zero = jnp.zeros((PAD, LANES), F32)
    for cp in copies[:2]:
        cp.wait()

    def conv_step(c, _):
        lanes = chunk(c)
        x = x_ref[:, lanes].astype(F32)
        padded = jnp.concatenate([zero, x * live, zero], axis=0)
        conv_ref[:, lanes] = x + conv_chunk(padded, taps_ref, lanes, rows, False)
        return 0

    lax.fori_loop(0, width // LANES, conv_step, 0)
    for cp in copies[2:]:
        cp.wait()


def edge_convs(low, high, taps_ref, lanes, reverse):
    zero = jnp.zeros((2 * PAD, LANES), F32)
    top = conv_chunk(jnp.concatenate([low, zero], axis=0), taps_ref, lanes, PAD, reverse)
    end = conv_chunk(jnp.concatenate([zero, high], axis=0), taps_ref, lanes, PAD, reverse)
    return top, end


def pre_kernel(
    len_ref, first_ref, conv_ref, near_ref, far_ref, taps_ref, gain_ref, w_ref, d_ref,
    send_ref, all_ref, mixed_ref, rstd_ref,
):
    rows, width = conv_ref.shape

    def conv_step(c, sq):
        lanes = chunk(c)
        low, high = ends(first_ref[0], near_ref, far_ref, lanes, rows, len_ref[0])
        top, end = edge_convs(low, high, taps_ref, lanes, False)
        mixed = jnp.concatenate(
            [
                conv_ref[:PAD, lanes] + top,
                conv_ref[PAD : rows - PAD, lanes],
                conv_ref[rows - PAD :, lanes] + end,
            ],
            axis=0,
        )
        mixed_ref[:, lanes] = mixed
        return sq + mixed * mixed

    sq = lax.fori_loop(0, width // LANES, conv_step, jnp.zeros((rows, LANES), F32))
    rstd = lax.rsqrt(jnp.sum(sq, axis=-1, keepdims=True) / width + 1e-05)
    rstd_ref[...] = jnp.broadcast_to(rstd, (rows, LANES))
    normed = (mixed_ref[...] * rstd * gain_ref[...]).astype(BF)
    for i in range(3):
        heads = jnp.dot(normed, w_ref[i], preferred_element_type=F32)
        heads = heads.T.astype(BF).reshape(HEADS, HDIM, rows)
        send_ref[:, i * HDIM : (i + 1) * HDIM, :] = heads
        all_ref[:, i * HDIM : (i + 1) * HDIM, :] = heads
    all_ref[:, 3 * HDIM :, :] = d_ref[...]


def attn_kernel(
    len_ref, late_ref, part_hbm, whole_hbm, d_hbm, out_ref, in_ref, qt_scr, dt_scr, kvt_scr, kv_scr,
    s_scr, e_scr, acc_scr, top_scr, sems, *, block, sstep, step,
):
    count, _, rows = in_ref.shape
    frames = count * rows
    length = len_ref[0]
    scale = HDIM ** (-0.5)
    factor = scale * math.log2(math.e)
    half = frames // 2
    steps = frames // step
    blocks = frames // block

    @pl.when(late_ref[0] == 0)
    def _():
        cp = pltpu.make_async_copy(whole_hbm, in_ref, sems.at[0])
        cp.start()
        cp.wait()

    @pl.when(late_ref[0] != 0)
    def _():
        first = pltpu.make_async_copy(part_hbm, in_ref.at[:, : 3 * HDIM], sems.at[0])
        second = pltpu.make_async_copy(d_hbm, in_ref.at[:, 3 * HDIM :], sems.at[1])
        first.start()
        second.start()
        first.wait()
        second.wait()

    for s in range(count):
        at = slice(s * rows, (s + 1) * rows)
        qt_scr[:, at] = in_ref[s, 0:HDIM, :]
        kvt = in_ref[s, HDIM : 3 * HDIM, :]
        kvt_scr[:, at] = kvt
        kv_scr[at, :] = kvt.T
        dt_scr[:, at] = in_ref[s, 3 * HDIM :, :]
    acc_scr[...] = jnp.zeros_like(acc_scr)
    zero = jnp.zeros((HDIM, block), BF)

    def masked_scores(first, rows, qt):
        s = jnp.dot(kv_scr[pl.ds(first, rows), :], qt, preferred_element_type=F32)
        pos = first + lax.broadcasted_iota(jnp.int32, (rows, block), 0)
        return jnp.where(pos < length, s, -1e30)

    def squares(ref, rows):
        return jnp.sum(jnp.square(ref[rows, :].astype(F32)), axis=0, keepdims=True)

    longest = jnp.max(squares(kvt_scr, slice(0, HDIM)), axis=-1, keepdims=True)
    bound = jnp.sqrt(squares(qt_scr, slice(0, HDIM)) * longest)
    top_scr[...] = bound
    in_range = jnp.max(bound) * (2 * factor) < 100.0

    @pl.when(jnp.logical_not(in_range))
    def _():
        def one(b, _):
            cols = pl.ds(pl.multiple_of(b * block, block), block)
            qt = jnp.concatenate([qt_scr[:, cols], zero], axis=0)

            def more(i, top):
                s = masked_scores(pl.multiple_of(i * rows, rows), rows, qt)
                return jnp.maximum(top, jnp.max(s, axis=0, keepdims=True))

            top = jnp.full((1, block), -1e30, F32)
            top_scr[:, cols] = lax.fori_loop(0, frames // rows, more, top)
            return 0

        lax.fori_loop(0, blocks, one, 0)

    none = jnp.zeros((HDIM, block), F32)

    def query(b):
        return jnp.concatenate([qt_scr[:, b * block : (b + 1) * block], zero], axis=0)

    def scores(b):
        qt = query(b)
        for i in range(frames // sstep):
            keys = slice(i * sstep, (i + 1) * sstep)
            if (i + 1) * sstep > half:
                s_scr[b % 2, keys, :] = masked_scores(i * sstep, sstep, qt)
            else:
                s_scr[b % 2, keys, :] = jnp.dot(kv_scr[keys, :], qt, preferred_element_type=F32)
        return top_scr[:, b * block : (b + 1) * block]

    def forward(b, i, top, total, out):
        keys = slice(i * step, (i + 1) * step)
        e = jnp.exp2((s_scr[b % 2, keys, :] - top) * factor)
        s_scr[b % 2, keys, :] = e
        eb = e.astype(BF)
        e_scr[b % 2, keys, :] = eb
        total = total + jnp.sum(e.reshape(step // 8, 8, block), axis=0)
        return total, out + jnp.dot(kvt_scr[HDIM:, keys], eb, preferred_element_type=F32)

    def between(b, total, out):
        inv = 1.0 / jnp.sum(total, axis=0, keepdims=True)
        out = out * inv
        dt = dt_scr[:, b * block : (b + 1) * block].astype(F32) * inv
        delta = jnp.sum(dt * out, axis=0, keepdims=True)
        return out, delta, jnp.concatenate([zero, dt.astype(BF)], axis=0)

    def backward(b, i, q0, d0, dt, delta, gq):
        keys = slice(i * step, (i + 1) * step)
        dp = jnp.dot(kv_scr[keys, :], dt, preferred_element_type=F32)
        ds = (s_scr[b % 2, keys, :] * (dp - delta)).astype(BF)
        acc_scr[keys, :] += jnp.dot(ds, q0, preferred_element_type=F32) + jnp.dot(
            e_scr[b % 2, keys, :], d0, preferred_element_type=F32
        )
        return gq + jnp.dot(kvt_scr[:HDIM, keys], ds, preferred_element_type=F32)

    state = None
    for b in range(blocks + 1):
        total, ahead, gq = jnp.zeros((8, block), F32), none, none
        if b < blocks:
            top = scores(b)
        if b > 0:
            out, delta, dt = state
            q0, d0 = query(b - 1).T, dt.T
        for i in range(steps):
            if b < blocks:
                total, ahead = forward(b, i, top, total, ahead)
            if b > 0:
                gq = backward(b - 1, i, q0, d0, dt, delta, gq)
        if b < blocks:
            state = between(b, total, ahead)
        if b > 0:
            gq = (gq * scale).astype(BF)
            out = out.astype(BF)
            for n in range(block // rows):
                at = slice(n * rows, (n + 1) * rows)
                dest = (b - 1) * (block // rows) + n
                out_ref[dest, 0:HDIM, :] = gq[:, at]
                out_ref[dest, 3 * HDIM : 4 * HDIM, :] = out[:, at]
    lane = lax.broadcasted_iota(jnp.int32, (rows, 2 * HDIM), 1)
    fix = jnp.where(lane < HDIM, scale, 1.0)
    for s in range(count):
        acc = acc_scr[s * rows : (s + 1) * rows, :]
        out_ref[s, HDIM : 3 * HDIM, :] = (acc * fix).astype(BF).T


def back_kernel(
    in_ref, wq_ref, wk_ref, wv_ref, mixed_ref, rstd_ref, gain_ref, gm_ref
):
    rows, width = mixed_ref.shape
    grad = None
    for i, w_ref in enumerate((wq_ref, wk_ref, wv_ref)):
        feats = in_ref[:, i * HDIM : (i + 1) * HDIM, :].reshape(HEADS * HDIM, rows)
        part = jnp.dot(w_ref[...], feats, preferred_element_type=F32)
        grad = part if grad is None else grad + part
    grad = grad.T
    scaled = grad * gain_ref[...]
    mixed = mixed_ref[...]
    rstd = rstd_ref[:, 0:1]
    mean = jnp.sum(scaled * mixed, axis=-1, keepdims=True) / width
    gm = rstd * scaled - mixed * (rstd * rstd * rstd * mean)
    gm_ref[...] = gm


def taps_terms(len_ref, first_ref, x_ref, near_ref, far_ref, gm_ref, lanes):
    rows = x_ref.shape[0]
    first = first_ref[0]
    low, high = ends(first, near_ref, far_ref, lanes, rows, len_ref[0])
    live = live_rows(first, rows, len_ref[0])
    padded = jnp.concatenate([low, x_ref[:, lanes].astype(F32) * live, high], axis=0)
    gm = gm_ref[:, lanes]
    result = [None] * (KSIZE + 1)
    for r in range(8):
        fill = [jnp.zeros((r, LANES), F32)] if r else []
        ext = jnp.concatenate(fill + [gm, jnp.zeros((8 - r, LANES), F32)], axis=0)
        for a in range(4):
            o = 8 * a + r
            if o == 0:
                continue
            prod = ext * padded[8 * a : 8 * a + rows + 8]
            result[o - 1] = jnp.sum(prod, axis=0, keepdims=True)
    result[KSIZE] = jnp.zeros((1, LANES), F32)
    return jnp.concatenate(result, axis=0)


def give_kernel(
    len_ref, first_ref, half_ref, x_ref, near_ref, far_ref, gm_ref, give_ref, edge_ref
):
    rows, width = x_ref.shape
    odd = lax.rem(first_ref[0] // rows, 2) == 1
    count = width // 2 // LANES

    def step(c, _):
        lanes = chunk(c + (1 - half_ref[0]) * count)
        give_ref[: KSIZE + 1, chunk(c)] = taps_terms(
            len_ref, first_ref, x_ref, near_ref, far_ref, gm_ref, lanes
        ).astype(BF)
        for n in range(2):
            lanes = chunk(c + n * count)
            head = gm_ref[:PAD, lanes]
            tail = gm_ref[rows - PAD :, lanes]
            at = n * PAD
            give_ref[KSIZE + 1 + at : KSIZE + 1 + at + PAD, chunk(c)] = jnp.where(
                odd, head, tail
            ).astype(BF)
            edge_ref[at : at + PAD, chunk(c)] = jnp.where(odd, tail, head).astype(BF)
        return 0

    lax.fori_loop(0, count, step, 0)


def keep_kernel(len_ref, first_ref, half_ref, x_ref, near_ref, far_ref, gm_ref, keep_ref):
    count = x_ref.shape[1] // 2 // LANES

    def step(c, _):
        keep_ref[:, chunk(c)] = taps_terms(
            len_ref, first_ref, x_ref, near_ref, far_ref, gm_ref, chunk(c + half_ref[0] * count)
        )
        return 0

    lax.fori_loop(0, count, step, 0)


def join_kernel(mine_ref, one_ref, two_ref, three_ref, edge_ref, out_ref):
    mine, one, two, three = (r[...].astype(F32) for r in (mine_ref, one_ref, two_ref, three_ref))
    out_ref[: KSIZE + 1] = ((mine + one) + (two + three)).astype(BF)
    out_ref[KSIZE + 1 :] = edge_ref[...]


def own_kernel(len_ref, first_ref, in_ref, gm_ref, taps_ref, attn_ref, own_ref):
    rows, width = gm_ref.shape
    live = live_rows(first_ref[0], rows, len_ref[0])
    zero = jnp.zeros((PAD, LANES), F32)

    def step(c, _):
        lanes = chunk(c)
        gm = gm_ref[:, lanes]
        padded = jnp.concatenate([zero, gm, zero], axis=0)
        own_ref[:, lanes] = gm + live * conv_chunk(padded, taps_ref, lanes, rows, True)
        return 0

    lax.fori_loop(0, width // LANES, step, 0)
    out = in_ref[:, 3 * HDIM : 4 * HDIM, :].reshape(HEADS * HDIM, rows).T
    attn_ref[...] = (out.astype(F32) * live[:, 0:1]).astype(BF)


def final_kernel(
    len_ref, first_ref, own_ref, near_ref, far_ref, taps_ref, gi_ref, *, frames,
):
    rows, width = own_ref.shape
    first = first_ref[0]
    live = live_rows(first, rows, len_ref[0])
    count = width // 2 // LANES

    def step(c, _):
        for n in range(2):
            lanes = chunk(c + n * count)
            at = KSIZE + 1 + n * PAD
            low, high = ends(
                first, near_ref.at[at : at + PAD], far_ref.at[at : at + PAD], chunk(c), rows, frames
            )
            top, end = edge_convs(low, high, taps_ref, lanes, True)
            gi_ref[:PAD, lanes] = (own_ref[:PAD, lanes] + live[:PAD] * top).astype(BF)
            gi_ref[PAD : rows - PAD, lanes] = own_ref[PAD : rows - PAD, lanes].astype(BF)
            gi_ref[rows - PAD :, lanes] = (
                own_ref[rows - PAD :, lanes] + live[rows - PAD :] * end
            ).astype(BF)
        return 0

    lax.fori_loop(0, count, step, 0)


def params(mib):
    return pltpu.CompilerParams(vmem_limit_bytes=mib << 20)


def cost(us):
    return pl.CostEstimate(flops=int(us * 1.1e9), bytes_accessed=1024, transcendentals=0)


def local(inputs, lengths, kernel, gain, q_weight, k_weight, v_weight, grad_attn):
    rows, width = inputs.shape
    count = lax.axis_size("seq")
    frames = rows * count
    feats = HEADS * HDIM
    sds = jax.ShapeDtypeStruct
    here = lax.axis_index("seq")
    odd = lax.rem(here, 2)
    first = (here * rows).astype(jnp.int32).reshape(1)
    gain = gain.reshape(1, width)

    def peer(mine, move):
        return lax.ppermute(mine, "seq", [(i, move(i)) for i in range(count)])

    def near(mine):
        return peer(mine, lambda i: i ^ 1)

    def far(mine):
        return peer(mine, lambda i: (i + 1 if i % 2 else i - 1) % count)

    a2a = functools.partial(
        lax.all_to_all, axis_name="seq", split_axis=0, concat_axis=0, tiled=True
    )
    slices = (
        lax.dynamic_slice_in_dim(inputs, odd * (rows - PAD), PAD),
        lax.dynamic_slice_in_dim(inputs, (1 - odd) * (rows - PAD), PAD),
    )
    for_far, for_near, after = lax.optimization_barrier(slices + (first,))
    x_far = far(for_far)
    x_near = near(for_near)

    def in_hbm(array):
        return pltpu.with_memory_space_constraint(array, pltpu.HBM)

    late = lax.rem(lax.axis_index("dp"), 4) >= 2
    douts = pl.pallas_call(
        dout_kernel,
        name="dout",
        out_shape=sds((feats, rows), BF),
        in_specs=[SMEM, SMEM, VMEM],
        out_specs=VMEM,
        compiler_params=params(4),
        cost_estimate=cost(1),
    )(lengths, after, in_hbm(grad_attn)).reshape(HEADS, HDIM, rows)
    douts = lax.cond(late, a2a, lambda d: d, douts)
    ready, douts = lax.optimization_barrier((first, douts))
    own, weights = pl.pallas_call(
        early_kernel,
        name="early",
        out_shape=(
            pltpu.VMEM((rows, width), F32),
            pltpu.VMEM((3, width, feats), BF),
        ),
        in_specs=[SMEM, SMEM] + [HBM] * 5,
        out_specs=(VMEM,) * 2,
        scratch_shapes=[
            pltpu.VMEM((rows, width), BF),
            pltpu.VMEM((KSIZE, width), F32),
            pltpu.SemaphoreType.DMA((5,)),
        ],
        compiler_params=params(16),
        cost_estimate=cost(6),
    )(lengths, ready, *(in_hbm(a) for a in (inputs, kernel, q_weight, k_weight, v_weight)))
    send, send_all, mixed, rstd = pl.pallas_call(
        pre_kernel,
        name="pre",
        out_shape=(
            sds((HEADS, 3 * HDIM, rows), BF),
            sds((HEADS, 4 * HDIM, rows), BF),
            sds((rows, width), F32),
            sds((rows, LANES), F32),
        ),
        in_specs=[SMEM, SMEM] + [VMEM] * 7,
        out_specs=(VMEM,) * 4,
        compiler_params=params(16),
        cost_estimate=cost(3),
    )(lengths, first, own, x_near, x_far, kernel, gain, weights, douts)

    block, sstep, step = 512, 1024, 512

    part, whole = lax.cond(
        late,
        lambda part, whole: lax.optimization_barrier((a2a(part), whole)),
        lambda part, whole: (part, a2a(whole)),
        send, send_all,
    )
    heads_out = pl.pallas_call(
        functools.partial(attn_kernel, block=block, sstep=sstep, step=step),
        name="attn",
        out_shape=sds((HEADS, 4 * HDIM, rows), BF),
        in_specs=[SMEM, SMEM] + [ANY] * 3,
        out_specs=VMEM,
        scratch_shapes=[
            pltpu.VMEM((HEADS, 4 * HDIM, rows), BF),
            pltpu.VMEM((HDIM, frames), BF),
            pltpu.VMEM((HDIM, frames), BF),
            pltpu.VMEM((2 * HDIM, frames), BF),
            pltpu.VMEM((frames, 2 * HDIM), BF),
            pltpu.VMEM((2, frames, block), F32),
            pltpu.VMEM((2, frames, block), BF),
            pltpu.VMEM((frames, 2 * HDIM), F32),
            pltpu.VMEM((1, frames), F32),
            pltpu.SemaphoreType.DMA((2,)),
        ],
        compiler_params=params(32),
        cost_estimate=cost(15),
    )(lengths, late.astype(jnp.int32).reshape(1), part, whole, douts)
    grads = a2a(heads_out)

    gm = pl.pallas_call(
        back_kernel,
        name="back",
        out_shape=sds((rows, width), F32),
        in_specs=[VMEM] * 7,
        out_specs=VMEM,
        compiler_params=params(16),
        cost_estimate=cost(4),
    )(grads, q_weight, k_weight, v_weight, mixed, rstd, gain)
    here, gm = lax.optimization_barrier((here, gm))
    half = ((here ^ (here >> 1)) & 1).astype(jnp.int32)
    given = (lengths, first, half.reshape(1), inputs, x_near, x_far, gm)
    give, edge = pl.pallas_call(
        give_kernel,
        name="give",
        out_shape=(
            sds((KSIZE + 1 + 2 * PAD, width // 2), BF),
            sds((2 * PAD, width // 2), BF),
        ),
        in_specs=[SMEM] * 3 + [VMEM] * 4,
        out_specs=(VMEM,) * 2,
        compiler_params=params(16),
        cost_estimate=cost(2),
    )(*given)
    keep = pl.pallas_call(
        keep_kernel,
        name="keep",
        out_shape=sds((KSIZE + 1, width // 2), F32),
        in_specs=[SMEM] * 3 + [VMEM] * 4,
        out_specs=VMEM,
        compiler_params=params(16),
        cost_estimate=cost(2),
    )(*given)

    got = near(give)
    mine = (keep + got[: KSIZE + 1].astype(F32)).astype(BF)
    parts = [peer(mine, lambda i: i ^ bits) for bits in (4, 8, 12)]
    joined = pl.pallas_call(
        join_kernel,
        name="join",
        out_shape=sds((KSIZE + 1 + 2 * PAD, width // 2), BF),
        in_specs=[VMEM] * 5,
        out_specs=VMEM,
        compiler_params=params(4),
        cost_estimate=cost(1),
    )(mine, *parts, edge)
    last = far(joined)
    attn, own_gi = pl.pallas_call(
        own_kernel,
        name="own",
        out_shape=(sds((rows, feats), BF), sds((rows, width), F32)),
        in_specs=[SMEM, SMEM] + [VMEM] * 3,
        out_specs=(VMEM,) * 2,
        compiler_params=params(16),
        cost_estimate=cost(3),
    )(lengths, first, grads, gm, kernel)
    mine = (joined[: KSIZE + 1].astype(F32) + last[: KSIZE + 1].astype(F32)).astype(BF)
    other = near(mine)
    grad_input = pl.pallas_call(
        functools.partial(final_kernel, frames=frames),
        name="final",
        out_shape=sds((rows, width), BF),
        in_specs=[SMEM, SMEM] + [VMEM] * 4,
        out_specs=VMEM,
        compiler_params=params(16),
        cost_estimate=cost(1),
    )(lengths, first, own_gi, got, last, kernel)
    left = jnp.where(half == 0, mine, other)
    right = jnp.where(half == 0, other, mine)
    grad_kernel = jnp.concatenate([left, right], axis=1)[:KSIZE].astype(F32)
    return (attn, grad_input, grad_kernel)


def solution(mesh):
    placed = (P(("dp", "seq"), None), P("dp"), P(), P(), P(), P(), P(), P(("dp", "seq"), None))
    return jax.shard_map(
        local,
        mesh=mesh,
        in_specs=placed,
        out_specs=(P(("dp", "seq"), None), P(("dp", "seq"), None), P("dp", None)),
        check_vma=False,
    )
```
